512 devices in a mesh: island: 8 (over x, y_hi), fsdp: 64 (over y_lo, z, core).
Axes of the slice: x: 4, y: 8 (y_hi: 2, y_lo: 4; y = y_hi * 4 + y_lo), z: 8, core: 2. Of those that a mesh axis runs over, the one named last changes fastest.
Arguments:
- act_t: bfloat16 [6144, 65536], P(None, ('island', 'fsdp')), may hold values from -6 to 6
- cotangent: bfloat16 [65536, 512], P(('island', 'fsdp')), may hold values from -0.06591797 to 0.06591797
- inner_params: float32 [8, 4, 6144, 512], P('island', None, 'fsdp'), may hold values from -6 to 6
- outer_params: float32 [6144, 512], P('fsdp'), may hold values from -6 to 6
- momentum: float32 [6144, 512], P('fsdp'), may hold values from -3 to 3
- frag_index: int32 [4], replicated, may hold values from 0 to 3, each once
Outputs:
- weight_grad: float32 [8, 6144, 512], P('island', 'fsdp')
- input_grad: bfloat16 [6144, 65536], P(None, ('island', 'fsdp'))
- new_params: float32 [6144, 512], P('fsdp')
- new_momentum: float32 [6144, 512], P('fsdp')
The draws below stay inside these ranges and needn't reach their ends.
Inputs may be any that keep to these rules, and one draw needn't show every extreme that they name: `frag_index`: each slot number appears once.
All inputs are finite; a program needn't handle non-finite values.
Results may differ from the reference program's by a relative error of at most 0.005.
Values may be sent and summed in bfloat16 or wider, within the bound.
A program may use at most 64 MiB of HBM per device.

```python
import jax
import jax.numpy as jnp
from jax import lax

DW = 6144
KV = 512
TOK_DEV = 128
SLOTS = 4
TOKENS = 65536
N_ISLAND = 8
N_FSDP = 64


def steps_of(key, dims, shards, least, high):
    gain, own = 1.0, jax.random.fold_in(key, 6)
    for dim, parts in shards:
        draws = jnp.exp(jax.random.uniform(jax.random.fold_in(own, dim), (parts,), jnp.float32, least / len(shards), high / len(shards)))
        gain = gain * jnp.repeat(draws, dims[dim] // parts).reshape([-1 if axis == dim else 1 for axis in range(len(dims))])
    return gain


def centred(stream_key, extent, spread, bound, cuts=(), kind=jnp.bfloat16):
    array = spread * jax.random.normal(stream_key, extent, jnp.float32)
    if cuts:
        array = array * steps_of(stream_key, extent, cuts, -0.22, 0.18)
    return jnp.clip(array, -bound, bound).astype(kind)


def setup_inputs(seed: int = 0) -> dict:
    key_of = jax.random.split(jax.random.key(seed), 7)
    act_t = centred(key_of[0], (DW, TOKENS), 1.0, 6.0, ((1, 512),))
    cotangent = centred(key_of[1], (TOKENS, KV), (1.0 / (TOK_DEV * N_FSDP) ** 0.5), 0.06591797, ((0, 512),))
    inner_params = centred(key_of[2], (N_ISLAND, SLOTS, DW, KV), 1.0, 6.0, ((0, 8), (2, 64)), jnp.float32)
    outer_params = centred(key_of[3], (DW, KV), 1.0, 6.0, ((0, 64),), jnp.float32)
    momentum = centred(key_of[4], (DW, KV), 0.5, 3.0, ((0, 64),), jnp.float32)
    frag_index = jax.random.permutation(key_of[5], SLOTS).astype(jnp.int32)
    return dict(act_t=act_t, cotangent=cotangent, inner_params=inner_params, outer_params=outer_params, momentum=momentum, frag_index=frag_index)


def reference(act_t, cotangent, inner_params, outer_params, momentum, frag_index):
    frag_slot = frag_index[0].astype(jnp.int32)
    train_slot = frag_index[1].astype(jnp.int32)
    tok_island = TOK_DEV * N_FSDP

    def per_island(island):
        start = (island * tok_island).astype(jnp.int32)
        inputs = lax.dynamic_slice_in_dim(act_t, start, tok_island, 1)
        grads_out = lax.dynamic_slice_in_dim(cotangent, start, tok_island, 0)
        weights = lax.dynamic_index_in_dim(inner_params[island], train_slot, 0, keepdims=False).astype(jnp.bfloat16)
        weight_grad = jnp.dot(inputs, grads_out, preferred_element_type=jnp.float32)
        input_grad = lax.dot_general(weights, grads_out, (((1,), (1,)), ((), ())), preferred_element_type=jnp.float32)
        return weight_grad, input_grad.astype(jnp.bfloat16)

    weight_grad, pieces = lax.map(per_island, jnp.arange(N_ISLAND, dtype=jnp.int32))
    input_grad = jnp.transpose(pieces, (1, 0, 2)).reshape(DW, N_ISLAND * tok_island)
    fragment = lax.dynamic_index_in_dim(inner_params, frag_slot, 1, keepdims=False)
    delta = jnp.sum((outer_params[None] - fragment) / float(N_ISLAND), axis=0)
    new_momentum = 0.9 * momentum + delta
    new_params = outer_params - 0.7 * (delta + 0.9 * new_momentum)
    return weight_grad, input_grad, new_params, new_momentum
```

```python
import jax
import jax.numpy as jnp
from jax import lax
from jax.experimental import pallas as pl
from jax.experimental.pallas import tpu as pltpu
from jax.sharding import PartitionSpec as P

MESH = pl.DeviceIdType.MESH
KV = 512
TOK = 128
ROWS = 96
NZ = 8
NX = 4
HALF = NZ // 2
DIRS = (1, -1)


def chain(d, h):
    return HALF if d == h else HALF - 1


MESSAGES = [(d, h, j) for d in range(2) for h in range(2) for j in range(HALF) if j < chain(d, h)]
SUMS = [(d, u, r) for d in range(2) for u in range(2) for r in range(HALF) if HALF - r <= chain(d, u)]


def kernel(
    frag, x_hbm, g_hbm, inner_hbm, outer_hbm, mom_hbm,
    wg_out, ig_out, par_out, newmom_out,
    inner_v, outer_v, mom_v, gbuf, gt, xbuf, wbuf, osend, rs_send, rs_recv, fin, fin_send, fin_recv,
    arw, ar_recv, ar_mid, ar_mid_recv, ar_tot,
    local_sem, w_sem, g_sem, ag_sem, x_sem, o_sem, rs_sem, fin_sem, ar_sem, own_sem,
):
    island = lax.axis_index("island")
    me = lax.axis_index("fsdp")
    core = lax.rem(me, 2)
    z = lax.rem(me // 2, NZ)
    y = me // (2 * NZ)
    u = y // 2
    p = lax.rem(y, 2)
    ix = island // 2
    iy = lax.rem(island, 2)

    def at(yy, zz, cc):
        return (island, (yy * NZ + zz) * 2 + cc)

    def zoff(o):
        return lax.rem(z + (o + NZ), NZ)

    y_pair = y + 1 - 2 * p
    quad = [None, at(y, z, 1 - core), at(y_pair, z, core), at(y_pair, z, 1 - core)]
    quad_pc = [(p, core), (p, 1 - core), (1 - p, core), (1 - p, 1 - core)]
    far = at(lax.rem(y + 2, 4), z, core)
    ring = [at(y, zoff(1), core), at(y, zoff(-1), core)]
    xs = [lax.rem(ix + k, NX) for k in range(NX)]
    xdev = [None] + [(xs[k] * 2 + iy, me) for k in range(1, NX)]
    ydev = (ix * 2 + 1 - iy, me)

    loads = [
        pltpu.make_async_copy(inner_hbm.at[0], inner_v, local_sem.at[0]),
        pltpu.make_async_copy(g_hbm, gbuf.at[0], local_sem.at[1]),
        pltpu.make_async_copy(x_hbm.at[:, p, :, core], xbuf.at[0], local_sem.at[2]),
        pltpu.make_async_copy(outer_hbm, outer_v, local_sem.at[3]),
        pltpu.make_async_copy(mom_hbm, mom_v, local_sem.at[4]),
    ]
    for c in loads:
        c.start()

    barrier = pltpu.get_barrier_semaphore()
    partners = quad[1:] + [far] + ring + xdev[1:] + [ydev]
    for dev in partners:
        pl.semaphore_signal(barrier, inc=1, device_id=dev, device_id_type=MESH)

    sent = []

    def remote(src, dst, sems, k, dev):
        return pltpu.make_async_remote_copy(
            src_ref=src, dst_ref=dst, send_sem=sems.at[0, k], recv_sem=sems.at[1, k],
            device_id=dev, device_id_type=MESH,
        )

    def start(c):
        c.start()
        sent.append(c)

    def c_w():
        return remote(wbuf.at[u, z], wbuf.at[u, z], w_sem, 0, far)

    def c_w_recv():
        return remote(wbuf.at[1 - u, z], wbuf.at[1 - u, z], w_sem, 0, far)

    def c_g(r):
        src, dst, dev = ((0, 1, quad[1]), (0, 2, quad[2]), (2, 3, quad[1]))[r - 1]
        return remote(gbuf.at[src], gbuf.at[dst], g_sem, r - 1, dev)

    def c_ag(d, h, j):
        uu = u if h == 0 else 1 - u
        zz = zoff(-DIRS[d] * j)
        return remote(wbuf.at[uu, zz], wbuf.at[uu, zz], ag_sem, MESSAGES.index((d, h, j)), ring[d])

    def c_ag_recv(d, h, j):
        uu = u if h == 0 else 1 - u
        zz = zoff(-DIRS[d] * (j + 1))
        return remote(wbuf.at[uu, zz], wbuf.at[uu, zz], ag_sem, MESSAGES.index((d, h, j)), ring[d])

    def c_x1():
        return remote(x_hbm.at[:, p, :, 1 - core], xbuf.at[1], x_sem, 0, quad[1])

    def c_x(r, o):
        pp, cc = quad_pc[r]
        zz = zoff(o)
        return remote(x_hbm.at[:, pp, zz, cc], xbuf.at[r, :, zz], x_sem, 1 + (r - 2) * NZ + o % NZ, quad[r])

    def c_o(r, o):
        zz = zoff(o)
        return remote(osend.at[r, o % NZ], ig_out.at[:, p, zz, core], o_sem, (r - 1) * NZ + o % NZ, quad[r])

    def c_o_recv(r, o):
        pp, cc = quad_pc[r]
        zz = zoff(o)
        return remote(osend.at[r, o % NZ], ig_out.at[:, pp, zz, cc], o_sem, (r - 1) * NZ + o % NZ, quad[r])

    def c_own(o):
        return pltpu.make_async_copy(osend.at[0, o % NZ], ig_out.at[:, p, zoff(o), core], own_sem.at[o % NZ])

    def c_rs(d, uu, r):
        k = SUMS.index((d, uu, r))
        return remote(rs_send.at[k], rs_recv.at[k], rs_sem, k, ring[d])

    def c_fin():
        return remote(fin_send.at[1 - u], fin_recv, fin_sem, 0, far)

    def c_ara(k):
        return remote(arw.at[xs[k]], ar_recv.at[k - 1], ar_sem, k - 1, xdev[k])

    def c_arb():
        return remote(ar_mid, ar_mid_recv, ar_sem, 3, ydev)

    def c_arc(k):
        return remote(ar_tot.at[ix], ar_tot.at[ix], ar_sem, 3 + k, xdev[k])

    def c_arc_recv(k):
        src = xs[NX - k]
        return remote(ar_tot.at[src], ar_tot.at[src], ar_sem, 3 + k, xdev[k])

    loads[0].wait()
    wbuf[u, z] = inner_v[frag[1]].astype(jnp.bfloat16)
    pl.semaphore_wait(barrier, len(partners))
    start(c_w())
    for d in range(2):
        start(c_ag(d, 0, 0))
    loads[1].wait()
    start(c_g(2))
    start(c_g(1))
    start(c_x1())
    for o in (4, 3, -3):
        for r in (2, 3):
            start(c_x(r, o))

    loads[3].wait()
    weighted = (outer_v[...] - inner_v[frag[0]]) / 8.0
    for k in range(NX):
        arw[k] = weighted[:, k * 128:(k + 1) * 128]
    for k in range(1, NX):
        start(c_ara(k))

    c_w_recv().wait_recv()
    for d in range(2):
        start(c_ag(d, 1, 0))

    c_g(2).wait_recv()
    start(c_g(3))
    c_g(1).wait_recv()
    c_g(3).wait_recv()
    g_all = gbuf[...].reshape(4 * TOK, KV)
    gt[...] = g_all.T
    loads[2].wait()
    c_x1().wait_recv()

    def partial(o):
        for r in (2, 3):
            c_x(r, o).wait_recv()
        zz = zoff(o)
        lhs = jnp.concatenate([xbuf[r, :, zz].reshape(2 * ROWS, TOK) for r in range(4)], axis=1)
        return jnp.dot(lhs, gbuf[...].reshape(4 * TOK, KV), preferred_element_type=jnp.float32)

    def send_sums(r):
        for d in range(2):
            o = DIRS[d] * (HALF - r)
            part = partial(o)
            for uu in sorted(range(2), key=lambda v: (d, v, r - 1) in SUMS):
                mine = part[uu * ROWS:(uu + 1) * ROWS]
                if (d, uu, r - 1) in SUMS:
                    c_rs(d, uu, r - 1).wait_recv()
                    mine = mine + rs_recv[SUMS.index((d, uu, r - 1))].astype(jnp.float32)
                rs_send[SUMS.index((d, uu, r))] = mine.astype(jnp.bfloat16)
                start(c_rs(d, uu, r))

    def forward(j):
        for h in range(2):
            for d in range(2):
                if (d, h, j - 1) in MESSAGES:
                    c_ag_recv(d, h, j - 1).wait_recv()
                if (d, h, j) in MESSAGES:
                    start(c_ag(d, h, j))

    def columns(o):
        zz = zoff(o)
        rows = wbuf[:, zz].reshape(2 * ROWS, KV)
        out = jnp.dot(rows, gt[...], preferred_element_type=jnp.float32).astype(jnp.bfloat16)
        for r in range(4):
            osend[r, o % NZ] = out[:, r * TOK:(r + 1) * TOK].reshape(2, ROWS, TOK)
        for r in (2, 3, 1):
            start(c_o(r, o))
        c_own(o).start()

    part = partial(4)
    for d in range(2):
        rs_send[SUMS.index((d, d, 0))] = part[d * ROWS:(d + 1) * ROWS].astype(jnp.bfloat16)
        start(c_rs(d, d, 0))
    for o in (2, -2):
        for r in (2, 3):
            start(c_x(r, o))
    forward(1)

    for k in range(1, NX):
        c_ara(k).wait_recv()
    ar_mid[...] = arw[ix] + ar_recv[0] + ar_recv[1] + ar_recv[2]
    start(c_arb())

    send_sums(1)
    for o in (1, -1, 0):
        for r in (2, 3):
            start(c_x(r, o))
    forward(2)
    columns(0)

    c_arb().wait_recv()
    ar_tot[ix] = ar_mid[...] + ar_mid_recv[...]
    for k in range(1, NX):
        start(c_arc(k))

    send_sums(2)
    forward(3)
    columns(1)
    columns(-1)
    send_sums(3)
    columns(2)
    columns(-2)

    part = partial(0)
    for uu in range(2):
        total = part[uu * ROWS:(uu + 1) * ROWS]
        for d in range(2):
            c_rs(d, uu, HALF - 1).wait_recv()
            total = total + rs_recv[SUMS.index((d, uu, HALF - 1))].astype(jnp.float32)
        fin[uu] = total
        fin_send[uu] = total.astype(jnp.bfloat16)
    start(c_fin())
    forward(4)
    columns(3)
    columns(-3)
    columns(4)

    for k in range(1, NX):
        c_arc_recv(k).wait_recv()
    loads[4].wait()
    for k in range(NX):
        cols = slice(k * 128, (k + 1) * 128)
        delta = ar_tot[k]
        new_momentum = 0.9 * mom_v[:, cols] + delta
        newmom_out[:, cols] = new_momentum
        par_out[:, cols] = outer_v[:, cols] - 0.7 * (delta + 0.9 * new_momentum)

    c_fin().wait_recv()
    wg_out[...] = fin[u] + fin_recv[...].astype(jnp.float32)
    for o in range(-3, 5):
        for r in (1, 2, 3):
            c_o_recv(r, o).wait_recv()
        c_own(o).wait()
    for c in sent:
        c.wait_send()


def local(act_t, cotangent, inner_params, outer_params, momentum, frag_index):
    bf16, f32 = jnp.bfloat16, jnp.float32
    any_space = pl.BlockSpec(memory_space=pl.ANY)
    vmem = pl.BlockSpec(memory_space=pltpu.VMEM)
    shape6 = (2, 2, NZ, 2, ROWS, TOK)
    dma = pltpu.SemaphoreType.DMA
    wg, ig, par, newmom = pl.pallas_call(
        kernel,
        out_shape=(
            jax.ShapeDtypeStruct((ROWS, KV), f32),
            jax.ShapeDtypeStruct(shape6, bf16),
            jax.ShapeDtypeStruct((ROWS, KV), f32),
            jax.ShapeDtypeStruct((ROWS, KV), f32),
        ),
        in_specs=[pl.BlockSpec(memory_space=pltpu.SMEM)] + [any_space] * 5,
        out_specs=(vmem, any_space, vmem, vmem),
        scratch_shapes=[
            pltpu.VMEM((4, ROWS, KV), f32),
            pltpu.VMEM((ROWS, KV), f32),
            pltpu.VMEM((ROWS, KV), f32),
            pltpu.VMEM((4, TOK, KV), bf16),
            pltpu.VMEM((KV, 4 * TOK), bf16),
            pltpu.VMEM((4, 2, NZ, ROWS, TOK), bf16),
            pltpu.VMEM((2, NZ, ROWS, KV), bf16),
            pltpu.VMEM((4, NZ, 2, ROWS, TOK), bf16),
            pltpu.VMEM((len(SUMS), ROWS, KV), bf16),
            pltpu.VMEM((len(SUMS), ROWS, KV), bf16),
            pltpu.VMEM((2, ROWS, KV), f32),
            pltpu.VMEM((2, ROWS, KV), bf16),
            pltpu.VMEM((ROWS, KV), bf16),
            pltpu.VMEM((NX, ROWS, 128), f32),
            pltpu.VMEM((NX - 1, ROWS, 128), f32),
            pltpu.VMEM((ROWS, 128), f32),
            pltpu.VMEM((ROWS, 128), f32),
            pltpu.VMEM((NX, ROWS, 128), f32),
            dma((5,)),
            dma((2, 1)),
            dma((2, 3)),
            dma((2, len(MESSAGES))),
            dma((2, 1 + 2 * NZ)),
            dma((2, 3 * NZ)),
            dma((2, len(SUMS))),
            dma((2, 1)),
            dma((2, 7)),
            dma((NZ,)),
        ],
        compiler_params=pltpu.CompilerParams(
            collective_id=0, has_side_effects=True, vmem_limit_bytes=40 * 2**20
        ),
        cost_estimate=pl.CostEstimate(flops=1700000000, bytes_accessed=6000000, transcendentals=0),
    )(
        frag_index,
        act_t.reshape(shape6),
        cotangent,
        inner_params,
        outer_params,
        momentum,
    )
    return wg[None], ig.reshape(act_t.shape), par, newmom


def solution(mesh):
    in_specs = (
        P(None, ("island", "fsdp")),
        P(("island", "fsdp"), None),
        P("island", None, "fsdp", None),
        P("fsdp", None),
        P("fsdp", None),
        P(),
    )
    out_specs = (
        P("island", "fsdp", None),
        P(None, ("island", "fsdp")),
        P("fsdp", None),
        P("fsdp", None),
    )
    return jax.shard_map(local, mesh=mesh, in_specs=in_specs, out_specs=out_specs, check_vma=False)
```

```python
import jax
import jax.numpy as jnp
from jax import lax
from jax.experimental import pallas as pl
from jax.experimental.pallas import tpu as pltpu
from jax.sharding import PartitionSpec as P

MESH = pl.DeviceIdType.MESH
KV = 512
TOK = 128
ROWS = 96
NZ = 8
NX = 4
HALF = NZ // 2
DIRS = (1, -1)


def chain(d, h):
    return HALF if d == h else HALF - 1


MESSAGES = [(d, h, j) for d in range(2) for h in range(2) for j in range(HALF) if j < chain(d, h)]
SUMS = [(d, h, r) for d in range(2) for h in range(2) for r in range(HALF) if HALF - r <= chain(d, h)]
PAIR = 64
REST = ROWS - PAIR

PLAN = (
    ("G", 1), ("G", 2), ("X1", 0), ("A0",), ("X1", 1), ("X", 1, 4), ("X", 1, 3), ("X", 1, -3), ("W",),
    ("X", 1, 2), ("X", 1, -2), ("R1",), ("GS",), ("s", 1, 1, 0), ("X0",), ("s", 0, 0, 0), ("s", 0, 1, 1),
    ("s", 1, 0, 1), ("G3",), ("GP",), ("S", 1, 1, 0), ("S", 0, 1, 1), ("X", 1, 1), ("X", 1, -1),
    ("X", 1, 0), ("X", 0, 4), ("F", 0, 0, 1), ("F", 1, 0, 1), ("s", 1, 1, 1), ("s", 0, 0, 1), ("FW",),
    ("S", 1, 1, 1), ("X", 0, 3), ("X", 0, -3), ("X", 0, 2), ("R2",), ("C", 0), ("F", 0, 0, 2),
    ("F", 1, 0, 2), ("s", 0, 1, 2), ("s", 1, 1, 2), ("s", 0, 0, 2), ("s", 1, 0, 2), ("S", 0, 1, 2),
    ("S", 1, 1, 2), ("X", 0, -2), ("X", 0, 1), ("X", 0, -1), ("X", 0, 0), ("F", 0, 1, 1), ("F", 1, 1, 1),
    ("C", -1), ("C", 1), ("R3",), ("S", 0, 0, 0), ("s", 0, 1, 3), ("s", 1, 1, 3), ("s", 0, 0, 3),
    ("s", 1, 0, 3), ("S", 0, 1, 3), ("S", 1, 1, 3), ("S", 1, 0, 1), ("S", 0, 0, 1), ("F", 0, 0, 3),
    ("F", 1, 0, 3), ("F", 0, 1, 2), ("F", 1, 1, 2), ("C", -2), ("C", 2), ("l", 1), ("l", 0), ("L", 1),
    ("S", 0, 0, 2), ("S", 1, 0, 2), ("F", 0, 1, 3), ("F", 1, 1, 3), ("F", 0, 0, 4), ("F", 1, 0, 4),
    ("C", -3), ("C", 3), ("S", 0, 0, 3), ("S", 1, 0, 3), ("F", 0, 1, 4), ("F", 1, 1, 4), ("C", 4), ("R4",),
    ("L", 0),
)


def kernel(
    frag, x_hbm, g_hbm, inner_hbm, outer_hbm, mom_hbm,
    wg_out, ig_out, par_out, newmom_out,
    inner_v, outer_v, mom_v, gbuf, gt, xbuf, xrest, wbuf, osend, rs_send, rs_recv, fin_send, fin_recv,
    ss_send, ss_recv, rest_tot, rest_send, rest_recv,
    arw, ar_recv, ar_mid, ar_mid_recv, ar_tot,
    local_sem, w_sem, g_sem, ag_sem, x_sem, o_sem, rs_sem, ss_sem, fin_sem, ar_sem,
):
    island = lax.axis_index("island")
    me = lax.axis_index("fsdp")
    core = lax.rem(me, 2)
    z = lax.rem(me // 2, NZ)
    y = me // (2 * NZ)
    u = y // 2
    p = lax.rem(y, 2)
    half = (u, 1 - u)
    ix = island // 2
    iy = lax.rem(island, 2)

    def at(yy, zz, cc):
        return (island, (yy * NZ + zz) * 2 + cc)

    def zoff(o):
        return lax.rem(z + (o + NZ), NZ)

    y_pair = y + 1 - 2 * p
    quad = [None, at(y, z, 1 - core), at(y_pair, z, core), at(y_pair, z, 1 - core)]
    quad_pc = [(p, core), (p, 1 - core), (1 - p, core), (1 - p, 1 - core)]
    far = at(lax.rem(y + 2, 4), z, core)
    cross = at(3 - y, z, core)
    ring = [at(y, zoff(1), core), at(y, zoff(-1), core)]
    xs = [lax.rem(ix + k, NX) for k in range(NX)]
    xdev = [None] + [(xs[k] * 2 + iy, me) for k in range(1, NX)]
    ydev = (ix * 2 + 1 - iy, me)

    loads = [
        pltpu.make_async_copy(inner_hbm.at[0], inner_v, local_sem.at[0]),
        pltpu.make_async_copy(g_hbm, gbuf.at[0], local_sem.at[1]),
        pltpu.make_async_copy(x_hbm.at[:, p, :, core], xbuf.at[0], local_sem.at[2]),
        pltpu.make_async_copy(outer_hbm, outer_v, local_sem.at[3]),
        pltpu.make_async_copy(mom_hbm, mom_v, local_sem.at[4]),
        pltpu.make_async_copy(x_hbm.at[:, 1 - p, :, core, PAIR:], xrest.at[0], local_sem.at[5]),
    ]
    for c in loads:
        c.start()

    barrier = pltpu.get_barrier_semaphore()
    partners = quad[1:] + [far, cross] + ring + xdev[1:] + [ydev]
    for dev in partners:
        pl.semaphore_signal(barrier, inc=1, device_id=dev, device_id_type=MESH)

    sent = []

    def remote(src, dst, sems, k, dev):
        return pltpu.make_async_remote_copy(
            src_ref=src, dst_ref=dst, send_sem=sems.at[0, k], recv_sem=sems.at[1, k],
            device_id=dev, device_id_type=MESH,
        )

    def start(c):
        c.start()
        sent.append(c)

    def c_w():
        return remote(wbuf.at[u, z], wbuf.at[u, z], w_sem, 0, far)

    def c_w_recv():
        return remote(wbuf.at[1 - u, z], wbuf.at[1 - u, z], w_sem, 0, far)

    def c_g(r):
        src, dst, dev = ((0, 1, quad[1]), (0, 2, quad[2]), (2, 3, quad[1]))[r - 1]
        return remote(gbuf.at[src], gbuf.at[dst], g_sem, r - 1, dev)

    def c_ag(d, h, j):
        zz = zoff(-DIRS[d] * j)
        return remote(wbuf.at[half[h], zz], wbuf.at[half[h], zz], ag_sem, MESSAGES.index((d, h, j)), ring[d])

    def c_ag_recv(d, h, j):
        zz = zoff(-DIRS[d] * (j + 1))
        return remote(wbuf.at[half[h], zz], wbuf.at[half[h], zz], ag_sem, MESSAGES.index((d, h, j)), ring[d])

    def c_x1(k):
        if k == 0:
            return remote(x_hbm.at[:, 1 - p, :, 1 - core, PAIR:], xrest.at[1], x_sem, 0, quad[1])
        return remote(x_hbm.at[:, p, :, 1 - core], xbuf.at[1], x_sem, 1, quad[1])

    def c_x(r, h, o):
        pp, cc = quad_pc[r]
        zz = zoff(o)
        k = 2 + ((r - 2) * 2 + h) * NZ + o % NZ
        rows = pl.ds(0, PAIR)
        return remote(x_hbm.at[half[h], pp, zz, cc, rows], xbuf.at[r, half[h], zz, rows], x_sem, k, quad[r])

    def c_o(r, o):
        zz = zoff(o)
        return remote(osend.at[r, o % NZ], ig_out.at[:, p, zz, core], o_sem, (r - 1) * NZ + o % NZ, quad[r])

    def c_o_recv(r, o):
        pp, cc = quad_pc[r]
        zz = zoff(o)
        return remote(osend.at[r, o % NZ], ig_out.at[:, pp, zz, cc], o_sem, (r - 1) * NZ + o % NZ, quad[r])

    def c_rs(d, h, r):
        k = SUMS.index((d, h, r))
        return remote(rs_send.at[k], rs_recv.at[k], rs_sem, k, ring[d])

    def c_ss(d, h, r):
        k = SUMS.index((d, h, r))
        return remote(ss_send.at[k], ss_recv.at[k], ss_sem, k, ring[d])

    def c_fin(k):
        if k == 0:
            return remote(fin_send, fin_recv, fin_sem, 0, far)
        src = rest_send.at[0, 1 - u] if k == 1 else rest_send.at[1, u if k == 2 else 1 - u]
        return remote(src, rest_recv.at[k - 1], fin_sem, k, (far, quad[2], cross)[k - 1])

    def c_ara(k):
        return remote(arw.at[xs[k]], ar_recv.at[k - 1], ar_sem, k - 1, xdev[k])

    def c_arb():
        return remote(ar_mid, ar_mid_recv, ar_sem, 3, ydev)

    def c_arc(k):
        return remote(ar_tot.at[ix], ar_tot.at[ix], ar_sem, 3 + k, xdev[k])

    def c_arc_recv(k):
        src = xs[NX - k]
        return remote(ar_tot.at[src], ar_tot.at[src], ar_sem, 3 + k, xdev[k])

    loads[0].wait()
    wbuf[u, z] = inner_v[frag[1]].astype(jnp.bfloat16)
    pl.semaphore_wait(barrier, len(partners))

    def product(lhs, members):
        g = gbuf[0:members].reshape(members * TOK, KV)
        return jnp.dot(lhs, g, preferred_element_type=jnp.float32)

    def pair_part(h, o):
        for r in (2, 3):
            c_x(r, h, o).wait_recv()
        return product(jnp.concatenate([xbuf[r, half[h], zoff(o), 0:PAIR] for r in range(4)], axis=1), 4)

    def rest_part(b, o):
        if b == 0:
            lhs = [xbuf[r, :, zoff(o), PAIR:ROWS] for r in range(2)]
        else:
            lhs = [xrest[r, :, zoff(o)] for r in range(2)]
        return product(jnp.concatenate([v.reshape(2 * REST, TOK) for v in lhs], axis=1), 2)

    def add_and_send(part, copy, send, recv, d, h, r):
        mine = part(h, DIRS[d] * (HALF - r))
        if (d, h, r - 1) in SUMS:
            copy(d, h, r - 1).wait_recv()
            mine = mine + recv[SUMS.index((d, h, r - 1))].astype(jnp.float32)
        send[SUMS.index((d, h, r))] = mine.astype(jnp.bfloat16)
        start(copy(d, h, r))

    def last_sum(part, copy, recv, h):
        total = part(h, 0)
        for d in range(2):
            copy(d, h, HALF - 1).wait_recv()
            total = total + recv[SUMS.index((d, h, HALF - 1))].astype(jnp.float32)
        return total

    def do(op, *i):
        if op == "A0":
            for d in range(2):
                start(c_ag(d, 0, 0))
        elif op == "W":
            start(c_w())
        elif op == "FW":
            c_w_recv().wait_recv()
            for d in range(2):
                start(c_ag(d, 1, 0))
        elif op == "G":
            start(c_g(i[0]))
        elif op == "X1":
            start(c_x1(i[0]))
        elif op == "GS":
            c_g(1).wait_recv()
            loads[5].wait()
            c_x1(0).wait_recv()
        elif op == "G3":
            c_g(2).wait_recv()
            start(c_g(3))
        elif op == "GP":
            c_g(3).wait_recv()
            gt[...] = gbuf[...].reshape(4 * TOK, KV).T
        elif op == "X0":
            loads[2].wait()
            c_x1(1).wait_recv()
        elif op == "X":
            for r in (2, 3):
                start(c_x(r, *i))
        elif op == "s":
            add_and_send(rest_part, c_ss, ss_send, ss_recv, *i)
        elif op == "S":
            add_and_send(pair_part, c_rs, rs_send, rs_recv, *i)
        elif op == "l":
            total = last_sum(rest_part, c_ss, ss_recv, i[0]).reshape(2, REST, KV)
            if i[0] == 0:
                rest_tot[...] = total
            rest_send[i[0]] = total.astype(jnp.bfloat16)
            for k in ((1,), (2, 3))[i[0]]:
                start(c_fin(k))
        elif op == "L":
            total = last_sum(pair_part, c_rs, rs_recv, i[0])
            if i[0] == 1:
                fin_send[...] = total.astype(jnp.bfloat16)
                start(c_fin(0))
            else:
                wg_out[0:PAIR] = total
        elif op == "F":
            d, h, j = i
            if (d, h, j - 1) in MESSAGES:
                c_ag_recv(d, h, j - 1).wait_recv()
            if (d, h, j) in MESSAGES:
                start(c_ag(d, h, j))
        elif op == "C":
            o = i[0]
            rows = wbuf[:, zoff(o)].reshape(2 * ROWS, KV)
            out = jnp.dot(rows, gt[...], preferred_element_type=jnp.float32).astype(jnp.bfloat16)
            for r in range(1, 4):
                osend[r, o % NZ] = out[:, r * TOK:(r + 1) * TOK].reshape(2, ROWS, TOK)
            for r in (2, 3, 1):
                start(c_o(r, o))
            ig_out[:, p, zoff(o), core] = out[:, :TOK].reshape(2, ROWS, TOK)
        elif op == "R1":
            loads[3].wait()
            weighted = (outer_v[...] - inner_v[frag[0]]) / 8.0
            for k in range(NX):
                arw[k] = weighted[:, k * 128:(k + 1) * 128]
            for k in range(1, NX):
                start(c_ara(k))
        elif op == "R2":
            for k in range(1, NX):
                c_ara(k).wait_recv()
            ar_mid[...] = arw[ix] + ar_recv[0] + ar_recv[1] + ar_recv[2]
            start(c_arb())
        elif op == "R3":
            c_arb().wait_recv()
            ar_tot[ix] = ar_mid[...] + ar_mid_recv[...]
            for k in range(1, NX):
                start(c_arc(k))
        elif op == "R4":
            for k in range(1, NX):
                c_arc_recv(k).wait_recv()
            loads[4].wait()
            for k in range(NX):
                cols = slice(k * 128, (k + 1) * 128)
                delta = ar_tot[k]
                new_momentum = 0.9 * mom_v[:, cols] + delta
                newmom_out[:, cols] = new_momentum
                par_out[:, cols] = outer_v[:, cols] - 0.7 * (delta + 0.9 * new_momentum)

    loads[1].wait()
    for step in PLAN:
        do(*step)

    for k in range(4):
        c_fin(k).wait_recv()
    wg_out[0:PAIR] += fin_recv[...].astype(jnp.float32)
    rest = rest_tot[u]
    for k in range(3):
        rest = rest + rest_recv[k].astype(jnp.float32)
    wg_out[PAIR:ROWS] = rest
    for o in range(-3, 5):
        for r in (1, 2, 3):
            c_o_recv(r, o).wait_recv()
    for c in sent:
        c.wait_send()


def local(act_t, cotangent, inner_params, outer_params, momentum, frag_index):
    bf16, f32 = jnp.bfloat16, jnp.float32
    hbm = pl.BlockSpec(memory_space=pltpu.HBM)
    vmem = pl.BlockSpec(memory_space=pltpu.VMEM)
    shape6 = (2, 2, NZ, 2, ROWS, TOK)
    dma = pltpu.SemaphoreType.DMA
    wg, ig, par, newmom = pl.pallas_call(
        kernel,
        out_shape=(
            pltpu.VMEM((ROWS, KV), f32),
            pltpu.VMEM(shape6, bf16),
            pltpu.VMEM((ROWS, KV), f32),
            pltpu.VMEM((ROWS, KV), f32),
        ),
        in_specs=[pl.BlockSpec(memory_space=pltpu.SMEM)] + [hbm] * 5,
        out_specs=(vmem, vmem, vmem, vmem),
        scratch_shapes=[
            pltpu.VMEM((4, ROWS, KV), f32),
            pltpu.VMEM((ROWS, KV), f32),
            pltpu.VMEM((ROWS, KV), f32),
            pltpu.VMEM((4, TOK, KV), bf16),
            pltpu.VMEM((KV, 4 * TOK), bf16),
            pltpu.VMEM((4, 2, NZ, ROWS, TOK), bf16),
            pltpu.VMEM((2, 2, NZ, REST, TOK), bf16),
            pltpu.VMEM((2, NZ, ROWS, KV), bf16),
            pltpu.VMEM((4, NZ, 2, ROWS, TOK), bf16),
            pltpu.VMEM((len(SUMS), PAIR, KV), bf16),
            pltpu.VMEM((len(SUMS), PAIR, KV), bf16),
            pltpu.VMEM((PAIR, KV), bf16),
            pltpu.VMEM((PAIR, KV), bf16),
            pltpu.VMEM((len(SUMS), 2 * REST, KV), bf16),
            pltpu.VMEM((len(SUMS), 2 * REST, KV), bf16),
            pltpu.VMEM((2, REST, KV), f32),
            pltpu.VMEM((2, 2, REST, KV), bf16),
            pltpu.VMEM((3, REST, KV), bf16),
            pltpu.VMEM((NX, ROWS, 128), f32),
            pltpu.VMEM((NX - 1, ROWS, 128), f32),
            pltpu.VMEM((ROWS, 128), f32),
            pltpu.VMEM((ROWS, 128), f32),
            pltpu.VMEM((NX, ROWS, 128), f32),
            dma((6,)),
            dma((2, 1)),
            dma((2, 3)),
            dma((2, len(MESSAGES))),
            dma((2, 2 + 4 * NZ)),
            dma((2, 3 * NZ)),
            dma((2, len(SUMS))),
            dma((2, len(SUMS))),
            dma((2, 4)),
            dma((2, 7)),
        ],
        compiler_params=pltpu.CompilerParams(
            collective_id=0, has_side_effects=True, vmem_limit_bytes=56 * 2**20
        ),
        cost_estimate=pl.CostEstimate(flops=1700000000, bytes_accessed=6000000, transcendentals=0),
    )(
        frag_index,
        act_t.reshape(shape6),
        cotangent,
        inner_params,
        outer_params,
        momentum,
    )
    return wg[None], ig.reshape(act_t.shape), par, newmom


def solution(mesh):
    in_specs = (
        P(None, ("island", "fsdp")),
        P(("island", "fsdp"), None),
        P("island", None, "fsdp", None),
        P("fsdp", None),
        P("fsdp", None),
        P(),
    )
    out_specs = (
        P("island", "fsdp", None),
        P(None, ("island", "fsdp")),
        P("fsdp", None),
        P("fsdp", None),
    )
    return jax.shard_map(local, mesh=mesh, in_specs=in_specs, out_specs=out_specs, check_vma=False)
```

```python
import jax
import jax.numpy as jnp
from jax import lax
from jax.experimental import pallas as pl
from jax.experimental.pallas import tpu as pltpu
from jax.sharding import PartitionSpec as P

MESH = pl.DeviceIdType.MESH
KV = 512
TOK = 128
ROWS = 96
NZ = 8
NX = 4
HALF = NZ // 2
DIRS = (1, -1)


def chain(d, h):
    return HALF if d == h else HALF - 1


MESSAGES = [(d, h, j) for d in range(2) for h in range(2) for j in range(HALF) if j < chain(d, h)]
SUMS = [(d, h, r) for d in range(2) for h in range(2) for r in range(HALF) if HALF - r <= chain(d, h)]
PAIR = 64
REST = ROWS - PAIR

PLAN = (
    ("X", 1, 4), ("A0",), ("G", 1), ("X1", 0), ("X", 1, -3), ("G", 2), ("X", 0, 3), ("W",), ("R1",),
    ("X", 0, -2), ("X1", 1), ("GS",), ("s", 0, 1, 1), ("s", 1, 1, 0), ("X0",), ("s", 0, 0, 0),
    ("s", 1, 0, 1), ("F", 0, 0, 1), ("F", 1, 0, 1), ("X", 1, 1), ("X", 1, 0), ("s", 0, 1, 2),
    ("s", 1, 1, 1), ("G3",), ("R2",), ("s", 0, 0, 1), ("GP",), ("S", 1, 1, 0), ("s", 1, 0, 2),
    ("F", 0, 0, 2), ("F", 1, 0, 2), ("X", 0, 2), ("X", 1, 2), ("s", 0, 1, 3), ("s", 1, 1, 2), ("X", 0, -1),
    ("X", 1, -1), ("FW",), ("s", 0, 0, 2), ("S", 1, 1, 1), ("X", 0, 0), ("C", 0), ("s", 1, 0, 3), ("R3",),
    ("F", 0, 0, 3), ("X", 1, 3), ("X", 0, 1), ("F", 1, 0, 3), ("X", 0, 4), ("s", 1, 1, 3), ("X", 0, -3),
    ("F", 0, 1, 1), ("C", -1), ("X", 1, -2), ("s", 0, 0, 3), ("R4",), ("S", 0, 1, 1), ("F", 1, 1, 1),
    ("C", 1), ("S", 0, 0, 0), ("F", 0, 0, 4), ("S", 1, 0, 1), ("F", 0, 1, 2), ("C", -2), ("l", 1),
    ("S", 1, 1, 2), ("l", 0), ("F", 1, 1, 2), ("C", 2), ("S", 0, 1, 2), ("S", 1, 0, 2), ("S", 0, 0, 1),
    ("S", 1, 1, 3), ("F", 0, 1, 3), ("C", -3), ("F", 1, 1, 3), ("C", 3), ("S", 0, 1, 3), ("S", 1, 0, 3),
    ("S", 0, 0, 2), ("L", 1), ("F", 1, 1, 4), ("C", 4), ("S", 0, 0, 3), ("L", 0),
)


def kernel(
    frag, x_hbm, g_hbm, inner_hbm, outer_hbm, mom_hbm,
    wg_out, ig_out, par_out, newmom_out,
    inner_v, outer_v, mom_v, gbuf, gt, xbuf, xrest, wbuf, osend, rs_send, rs_recv, fin_send, fin_recv,
    ss_send, ss_recv, rest_tot, rest_send, rest_recv,
    arw, ar_recv, ar_mid, ar_mid_recv, ar_tot,
    local_sem, w_sem, g_sem, ag_sem, x_sem, o_sem, rs_sem, ss_sem, fin_sem, ar_sem,
):
    island = lax.axis_index("island")
    me = lax.axis_index("fsdp")
    core = lax.rem(me, 2)
    z = lax.rem(me // 2, NZ)
    y = me // (2 * NZ)
    u = y // 2
    p = lax.rem(y, 2)
    half = (u, 1 - u)
    ix = island // 2
    iy = lax.rem(island, 2)

    def at(yy, zz, cc):
        return (island, (yy * NZ + zz) * 2 + cc)

    def zoff(o):
        return lax.rem(z + (o + NZ), NZ)

    y_pair = y + 1 - 2 * p
    quad = [None, at(y, z, 1 - core), at(y_pair, z, core), at(y_pair, z, 1 - core)]
    quad_pc = [(p, core), (p, 1 - core), (1 - p, core), (1 - p, 1 - core)]
    far = at(lax.rem(y + 2, 4), z, core)
    cross = at(3 - y, z, core)
    ring = [at(y, zoff(1), core), at(y, zoff(-1), core)]
    xs = [lax.rem(ix + k, NX) for k in range(NX)]
    xdev = [None] + [(xs[k] * 2 + iy, me) for k in range(1, NX)]
    ydev = (ix * 2 + 1 - iy, me)

    loads = [
        pltpu.make_async_copy(inner_hbm.at[0], inner_v, local_sem.at[0]),
        pltpu.make_async_copy(g_hbm, gbuf.at[0], local_sem.at[1]),
        pltpu.make_async_copy(x_hbm.at[:, p, :, core], xbuf.at[0], local_sem.at[2]),
        pltpu.make_async_copy(outer_hbm, outer_v, local_sem.at[3]),
        pltpu.make_async_copy(mom_hbm, mom_v, local_sem.at[4]),
        pltpu.make_async_copy(x_hbm.at[:, 1 - p, :, core, PAIR:], xrest.at[0], local_sem.at[5]),
    ]
    for c in loads:
        c.start()

    barrier = pltpu.get_barrier_semaphore()
    partners = quad[1:] + [far, cross] + ring + xdev[1:] + [ydev]
    for dev in partners:
        pl.semaphore_signal(barrier, inc=1, device_id=dev, device_id_type=MESH)

    sent = []

    def remote(src, dst, sems, k, dev):
        return pltpu.make_async_remote_copy(
            src_ref=src, dst_ref=dst, send_sem=sems.at[0, k], recv_sem=sems.at[1, k],
            device_id=dev, device_id_type=MESH,
        )

    def start(c):
        c.start()
        sent.append(c)

    def c_w():
        return remote(wbuf.at[u, z], wbuf.at[u, z], w_sem, 0, far)

    def c_w_recv():
        return remote(wbuf.at[1 - u, z], wbuf.at[1 - u, z], w_sem, 0, far)

    def c_g(r):
        src, dst, dev = ((0, 1, quad[1]), (0, 2, quad[2]), (2, 3, quad[1]))[r - 1]
        return remote(gbuf.at[src], gbuf.at[dst], g_sem, r - 1, dev)

    def c_ag(d, h, j):
        zz = zoff(-DIRS[d] * j)
        return remote(wbuf.at[half[h], zz], wbuf.at[half[h], zz], ag_sem, MESSAGES.index((d, h, j)), ring[d])

    def c_ag_recv(d, h, j):
        zz = zoff(-DIRS[d] * (j + 1))
        return remote(wbuf.at[half[h], zz], wbuf.at[half[h], zz], ag_sem, MESSAGES.index((d, h, j)), ring[d])

    def c_x1(k):
        if k == 0:
            return remote(x_hbm.at[:, 1 - p, :, 1 - core, PAIR:], xrest.at[1], x_sem, 0, quad[1])
        return remote(x_hbm.at[:, p, :, 1 - core], xbuf.at[1], x_sem, 1, quad[1])

    def c_x(r, h, o):
        pp, cc = quad_pc[r]
        zz = zoff(o)
        k = 2 + ((r - 2) * 2 + h) * NZ + o % NZ
        rows = pl.ds(0, PAIR)
        return remote(x_hbm.at[half[h], pp, zz, cc, rows], xbuf.at[r, half[h], zz, rows], x_sem, k, quad[r])

    def c_o(r, o):
        zz = zoff(o)
        return remote(osend.at[r, o % NZ], ig_out.at[:, p, zz, core], o_sem, (r - 1) * NZ + o % NZ, quad[r])

    def c_o_recv(r, o):
        pp, cc = quad_pc[r]
        zz = zoff(o)
        return remote(osend.at[r, o % NZ], ig_out.at[:, pp, zz, cc], o_sem, (r - 1) * NZ + o % NZ, quad[r])

    def c_rs(d, h, r):
        k = SUMS.index((d, h, r))
        return remote(rs_send.at[k], rs_recv.at[k], rs_sem, k, ring[d])

    def c_ss(d, h, r):
        k = SUMS.index((d, h, r))
        return remote(ss_send.at[k], ss_recv.at[k], ss_sem, k, ring[d])

    def c_fin(k):
        if k == 0:
            return remote(fin_send, fin_recv, fin_sem, 0, far)
        src = rest_send.at[0, 1 - u] if k == 1 else rest_send.at[1, u if k == 2 else 1 - u]
        return remote(src, rest_recv.at[k - 1], fin_sem, k, (far, quad[2], cross)[k - 1])

    def c_ara(k):
        return remote(arw.at[xs[k]], ar_recv.at[k - 1], ar_sem, k - 1, xdev[k])

    def c_arb():
        return remote(ar_mid, ar_mid_recv, ar_sem, 3, ydev)

    def c_arc(k):
        return remote(ar_tot.at[ix], ar_tot.at[ix], ar_sem, 3 + k, xdev[k])

    def c_arc_recv(k):
        src = xs[NX - k]
        return remote(ar_tot.at[src], ar_tot.at[src], ar_sem, 3 + k, xdev[k])

    loads[0].wait()
    wbuf[u, z] = inner_v[frag[1]].astype(jnp.bfloat16)
    pl.semaphore_wait(barrier, len(partners))

    def product(lhs, members):
        g = gbuf[0:members].reshape(members * TOK, KV)
        return jnp.dot(lhs, g, preferred_element_type=jnp.float32)

    def pair_part(h, o):
        for r in (2, 3):
            c_x(r, h, o).wait_recv()
        return product(jnp.concatenate([xbuf[r, half[h], zoff(o), 0:PAIR] for r in range(4)], axis=1), 4)

    def rest_part(b, o):
        if b == 0:
            lhs = [xbuf[r, :, zoff(o), PAIR:ROWS] for r in range(2)]
        else:
            lhs = [xrest[r, :, zoff(o)] for r in range(2)]
        return product(jnp.concatenate([v.reshape(2 * REST, TOK) for v in lhs], axis=1), 2)

    def add_and_send(part, copy, send, recv, d, h, r):
        mine = part(h, DIRS[d] * (HALF - r))
        if (d, h, r - 1) in SUMS:
            copy(d, h, r - 1).wait_recv()
            mine = mine + recv[SUMS.index((d, h, r - 1))].astype(jnp.float32)
        send[SUMS.index((d, h, r))] = mine.astype(jnp.bfloat16)
        start(copy(d, h, r))

    def last_sum(part, copy, recv, h):
        total = part(h, 0)
        for d in range(2):
            copy(d, h, HALF - 1).wait_recv()
            total = total + recv[SUMS.index((d, h, HALF - 1))].astype(jnp.float32)
        return total

    def do(op, *i):
        if op == "A0":
            for d in range(2):
                start(c_ag(d, 0, 0))
        elif op == "W":
            start(c_w())
        elif op == "FW":
            c_w_recv().wait_recv()
            for d in range(2):
                start(c_ag(d, 1, 0))
        elif op == "G":
            start(c_g(i[0]))
        elif op == "X1":
            start(c_x1(i[0]))
        elif op == "GS":
            c_g(1).wait_recv()
            loads[5].wait()
            c_x1(0).wait_recv()
        elif op == "G3":
            c_g(2).wait_recv()
            start(c_g(3))
        elif op == "GP":
            c_g(3).wait_recv()
            gt[...] = gbuf[...].reshape(4 * TOK, KV).T
        elif op == "X0":
            loads[2].wait()
            c_x1(1).wait_recv()
        elif op == "X":
            for r in (2, 3):
                start(c_x(r, *i))
        elif op == "s":
            add_and_send(rest_part, c_ss, ss_send, ss_recv, *i)
        elif op == "S":
            add_and_send(pair_part, c_rs, rs_send, rs_recv, *i)
        elif op == "l":
            total = last_sum(rest_part, c_ss, ss_recv, i[0]).reshape(2, REST, KV)
            if i[0] == 0:
                rest_tot[...] = total
            rest_send[i[0]] = total.astype(jnp.bfloat16)
            for k in ((1,), (2, 3))[i[0]]:
                start(c_fin(k))
        elif op == "L":
            total = last_sum(pair_part, c_rs, rs_recv, i[0])
            if i[0] == 1:
                fin_send[...] = total.astype(jnp.bfloat16)
                start(c_fin(0))
            else:
                wg_out[0:PAIR] = total
        elif op == "F":
            d, h, j = i
            if (d, h, j - 1) in MESSAGES:
                c_ag_recv(d, h, j - 1).wait_recv()
            if (d, h, j) in MESSAGES:
                start(c_ag(d, h, j))
        elif op == "C":
            o = i[0]
            rows = wbuf[:, zoff(o)].reshape(2 * ROWS, KV)
            out = jnp.dot(rows, gt[...], preferred_element_type=jnp.float32).astype(jnp.bfloat16)
            for r in range(1, 4):
                osend[r, o % NZ] = out[:, r * TOK:(r + 1) * TOK].reshape(2, ROWS, TOK)
            for r in (2, 3, 1):
                start(c_o(r, o))
            ig_out[:, p, zoff(o), core] = out[:, :TOK].reshape(2, ROWS, TOK)
        elif op == "R1":
            loads[3].wait()
            weighted = (outer_v[...] - inner_v[frag[0]]) / 8.0
            for k in range(NX):
                arw[k] = weighted[:, k * 128:(k + 1) * 128]
            for k in range(1, NX):
                start(c_ara(k))
        elif op == "R2":
            for k in range(1, NX):
                c_ara(k).wait_recv()
            ar_mid[...] = arw[ix] + ar_recv[0] + ar_recv[1] + ar_recv[2]
            start(c_arb())
        elif op == "R3":
            c_arb().wait_recv()
            ar_tot[ix] = ar_mid[...] + ar_mid_recv[...]
            for k in range(1, NX):
                start(c_arc(k))
        elif op == "R4":
            for k in range(1, NX):
                c_arc_recv(k).wait_recv()
            loads[4].wait()
            for k in range(NX):
                cols = slice(k * 128, (k + 1) * 128)
                delta = ar_tot[k]
                new_momentum = 0.9 * mom_v[:, cols] + delta
                newmom_out[:, cols] = new_momentum
                par_out[:, cols] = outer_v[:, cols] - 0.7 * (delta + 0.9 * new_momentum)

    loads[1].wait()
    for step in PLAN:
        do(*step)

    for k in range(4):
        c_fin(k).wait_recv()
    wg_out[0:PAIR] += fin_recv[...].astype(jnp.float32)
    rest = rest_tot[u]
    for k in range(3):
        rest = rest + rest_recv[k].astype(jnp.float32)
    wg_out[PAIR:ROWS] = rest
    for o in range(-3, 5):
        for r in (1, 2, 3):
            c_o_recv(r, o).wait_recv()
    for c in sent:
        c.wait_send()


def local(act_t, cotangent, inner_params, outer_params, momentum, frag_index):
    bf16, f32 = jnp.bfloat16, jnp.float32
    hbm = pl.BlockSpec(memory_space=pltpu.HBM)
    vmem = pl.BlockSpec(memory_space=pltpu.VMEM)
    shape6 = (2, 2, NZ, 2, ROWS, TOK)
    dma = pltpu.SemaphoreType.DMA
    wg, ig, par, newmom = pl.pallas_call(
        kernel,
        out_shape=(
            pltpu.VMEM((ROWS, KV), f32),
            pltpu.VMEM(shape6, bf16),
            pltpu.VMEM((ROWS, KV), f32),
            pltpu.VMEM((ROWS, KV), f32),
        ),
        in_specs=[pl.BlockSpec(memory_space=pltpu.SMEM)] + [hbm] * 5,
        out_specs=(vmem, vmem, vmem, vmem),
        scratch_shapes=[
            pltpu.VMEM((4, ROWS, KV), f32),
            pltpu.VMEM((ROWS, KV), f32),
            pltpu.VMEM((ROWS, KV), f32),
            pltpu.VMEM((4, TOK, KV), bf16),
            pltpu.VMEM((KV, 4 * TOK), bf16),
            pltpu.VMEM((4, 2, NZ, ROWS, TOK), bf16),
            pltpu.VMEM((2, 2, NZ, REST, TOK), bf16),
            pltpu.VMEM((2, NZ, ROWS, KV), bf16),
            pltpu.VMEM((4, NZ, 2, ROWS, TOK), bf16),
            pltpu.VMEM((len(SUMS), PAIR, KV), bf16),
            pltpu.VMEM((len(SUMS), PAIR, KV), bf16),
            pltpu.VMEM((PAIR, KV), bf16),
            pltpu.VMEM((PAIR, KV), bf16),
            pltpu.VMEM((len(SUMS), 2 * REST, KV), bf16),
            pltpu.VMEM((len(SUMS), 2 * REST, KV), bf16),
            pltpu.VMEM((2, REST, KV), f32),
            pltpu.VMEM((2, 2, REST, KV), bf16),
            pltpu.VMEM((3, REST, KV), bf16),
            pltpu.VMEM((NX, ROWS, 128), f32),
            pltpu.VMEM((NX - 1, ROWS, 128), f32),
            pltpu.VMEM((ROWS, 128), f32),
            pltpu.VMEM((ROWS, 128), f32),
            pltpu.VMEM((NX, ROWS, 128), f32),
            dma((6,)),
            dma((2, 1)),
            dma((2, 3)),
            dma((2, len(MESSAGES))),
            dma((2, 2 + 4 * NZ)),
            dma((2, 3 * NZ)),
            dma((2, len(SUMS))),
            dma((2, len(SUMS))),
            dma((2, 4)),
            dma((2, 7)),
        ],
        compiler_params=pltpu.CompilerParams(
            collective_id=0, has_side_effects=True, vmem_limit_bytes=56 * 2**20
        ),
        cost_estimate=pl.CostEstimate(flops=1700000000, bytes_accessed=6000000, transcendentals=0),
    )(
        frag_index,
        act_t.reshape(shape6),
        cotangent,
        inner_params,
        outer_params,
        momentum,
    )
    return wg[None], ig.reshape(act_t.shape), par, newmom


def solution(mesh):
    in_specs = (
        P(None, ("island", "fsdp")),
        P(("island", "fsdp"), None),
        P("island", None, "fsdp", None),
        P("fsdp", None),
        P("fsdp", None),
        P(),
    )
    out_specs = (
        P("island", "fsdp", None),
        P(None, ("island", "fsdp")),
        P("fsdp", None),
        P("fsdp", None),
    )
    return jax.shard_map(local, mesh=mesh, in_specs=in_specs, out_specs=out_specs, check_vma=False)
```

```python
import jax
import jax.numpy as jnp
from jax import lax
from jax.experimental import pallas as pl
from jax.experimental.pallas import tpu as pltpu
from jax.sharding import PartitionSpec as P

MESH = pl.DeviceIdType.MESH
KV = 512
TOK = 128
ROWS = 96
NZ = 8
NX = 4
HALF = NZ // 2
DIRS = (1, -1)


def chain(d, h):
    return HALF if d == h else HALF - 1


MESSAGES = [(d, h, j) for d in range(2) for h in range(2) for j in range(HALF) if j < chain(d, h)]
SUMS = [(d, h, r) for d in range(2) for h in range(2) for r in range(HALF) if HALF - r <= chain(d, h)]
PAIR = 64
REST = ROWS - PAIR

PLAN = (
    ("W",), ("G", 1), ("A0",), ("X1", 0), ("X", 0, 3), ("G", 2), ("X1", 1), ("X", 1, 4), ("X", 0, -3),
    ("GS",), ("s", 1, 1, 0), ("s", 0, 1, 1), ("X0",), ("s", 1, 0, 1), ("s", 0, 0, 0), ("F", 0, 0, 1),
    ("F", 1, 0, 1), ("X", 1, 0), ("R1",), ("s", 1, 1, 1), ("X", 0, 4), ("FW",), ("X", 0, 1), ("s", 1, 0, 2),
    ("X", 0, -2), ("G3",), ("s", 0, 0, 1), ("X", 1, -3), ("X", 1, 3), ("GP",), ("s", 0, 1, 2), ("X", 1, -1),
    ("s", 1, 1, 2), ("F", 0, 1, 1), ("S", 1, 1, 0), ("C", 0), ("S", 0, 0, 0), ("X", 1, 2), ("s", 1, 0, 3),
    ("X", 1, -2), ("X", 0, 2), ("s", 0, 0, 2), ("F", 1, 1, 1), ("F", 0, 0, 2), ("S", 0, 1, 1), ("C", 1),
    ("F", 0, 1, 2), ("S", 1, 1, 1), ("C", -2), ("C", -1), ("X", 0, 0), ("F", 1, 0, 2), ("F", 1, 1, 2),
    ("X", 1, 1), ("R2",), ("s", 0, 1, 3), ("S", 0, 1, 2), ("X", 0, -1), ("s", 1, 1, 3), ("S", 1, 1, 2),
    ("s", 0, 0, 3), ("S", 1, 0, 1), ("F", 1, 0, 3), ("C", 2), ("S", 0, 0, 1), ("F", 1, 1, 3),
    ("F", 0, 1, 3), ("C", 3), ("F", 0, 0, 3), ("C", -3), ("S", 0, 1, 3), ("S", 1, 1, 3), ("R3",),
    ("S", 1, 0, 2), ("l", 0), ("S", 0, 0, 2), ("l", 1), ("F", 1, 1, 4), ("F", 0, 0, 4), ("L", 1), ("C", 4),
    ("S", 0, 0, 3), ("S", 1, 0, 3), ("R4",), ("L", 0),
)


def kernel(
    frag, x_hbm, g_hbm, inner_hbm, outer_hbm, mom_hbm,
    f_out, ig_out,
    inner_v, outer_v, mom_v, gbuf, gt, xbuf, xrest, wbuf, osend, rs_send, rs_recv, fin_send, fin_recv,
    ss_send, ss_recv, rest_tot, rest_send, rest_recv,
    arw, ar_recv, ar_mid, ar_mid_recv, ar_tot,
    local_sem, w_sem, g_sem, ag_sem, x_sem, o_sem, rs_sem, ss_sem, fin_sem, ar_sem,
):
    wg_out, par_out, newmom_out = (f_out.at[k] for k in range(3))
    island = lax.axis_index("island")
    me = lax.axis_index("fsdp")
    core = lax.rem(me, 2)
    z = lax.rem(me // 2, NZ)
    y = me // (2 * NZ)
    u = y // 2
    p = lax.rem(y, 2)
    half = (u, 1 - u)
    ix = island // 2
    iy = lax.rem(island, 2)

    def at(yy, zz, cc):
        return (island, (yy * NZ + zz) * 2 + cc)

    def zoff(o):
        return lax.rem(z + (o + NZ), NZ)

    y_pair = y + 1 - 2 * p
    quad = [None, at(y, z, 1 - core), at(y_pair, z, core), at(y_pair, z, 1 - core)]
    quad_pc = [(p, core), (p, 1 - core), (1 - p, core), (1 - p, 1 - core)]
    far = at(lax.rem(y + 2, 4), z, core)
    cross = at(3 - y, z, core)
    ring = [at(y, zoff(1), core), at(y, zoff(-1), core)]
    xs = [lax.rem(ix + k, NX) for k in range(NX)]
    xdev = [None] + [(xs[k] * 2 + iy, me) for k in range(1, NX)]
    ydev = (ix * 2 + 1 - iy, me)

    loads = [
        pltpu.make_async_copy(inner_hbm.at[0], inner_v, local_sem.at[0]),
        pltpu.make_async_copy(g_hbm, gbuf.at[0], local_sem.at[1]),
        pltpu.make_async_copy(x_hbm.at[:, p, :, core], xbuf.at[0], local_sem.at[2]),
        pltpu.make_async_copy(outer_hbm, outer_v, local_sem.at[3]),
        pltpu.make_async_copy(mom_hbm, mom_v, local_sem.at[4]),
        pltpu.make_async_copy(x_hbm.at[:, 1 - p, :, core, PAIR:], xrest.at[0], local_sem.at[5]),
    ]
    for c in loads:
        c.start()

    barrier = pltpu.get_barrier_semaphore()
    partners = quad[1:] + [far, cross] + ring + xdev[1:] + [ydev]
    for dev in partners:
        pl.semaphore_signal(barrier, inc=1, device_id=dev, device_id_type=MESH)

    sent = []

    def remote(src, dst, sems, k, dev):
        return pltpu.make_async_remote_copy(
            src_ref=src, dst_ref=dst, send_sem=sems.at[0, k], recv_sem=sems.at[1, k],
            device_id=dev, device_id_type=MESH,
        )

    def start(c):
        c.start()
        sent.append(c)

    def c_w():
        return remote(wbuf.at[u, z], wbuf.at[u, z], w_sem, 0, far)

    def c_w_recv():
        return remote(wbuf.at[1 - u, z], wbuf.at[1 - u, z], w_sem, 0, far)

    def c_g(r):
        src, dst, dev = ((0, 1, quad[1]), (0, 2, quad[2]), (2, 3, quad[1]))[r - 1]
        return remote(gbuf.at[src], gbuf.at[dst], g_sem, r - 1, dev)

    def c_ag(d, h, j):
        zz = zoff(-DIRS[d] * j)
        return remote(wbuf.at[half[h], zz], wbuf.at[half[h], zz], ag_sem, MESSAGES.index((d, h, j)), ring[d])

    def c_ag_recv(d, h, j):
        zz = zoff(-DIRS[d] * (j + 1))
        return remote(wbuf.at[half[h], zz], wbuf.at[half[h], zz], ag_sem, MESSAGES.index((d, h, j)), ring[d])

    def c_x1(k):
        if k == 0:
            return remote(x_hbm.at[:, 1 - p, :, 1 - core, PAIR:], xrest.at[1], x_sem, 0, quad[1])
        return remote(x_hbm.at[:, p, :, 1 - core], xbuf.at[1], x_sem, 1, quad[1])

    def c_x(r, h, o):
        pp, cc = quad_pc[r]
        zz = zoff(o)
        k = 2 + ((r - 2) * 2 + h) * NZ + o % NZ
        rows = pl.ds(0, PAIR)
        return remote(x_hbm.at[half[h], pp, zz, cc, rows], xbuf.at[r, half[h], zz, rows], x_sem, k, quad[r])

    def c_o(r, o):
        zz = zoff(o)
        return remote(osend.at[r, o % NZ], ig_out.at[:, p, zz, core], o_sem, (r - 1) * NZ + o % NZ, quad[r])

    def c_o_recv(r, o):
        pp, cc = quad_pc[r]
        zz = zoff(o)
        return remote(osend.at[r, o % NZ], ig_out.at[:, pp, zz, cc], o_sem, (r - 1) * NZ + o % NZ, quad[r])

    def c_rs(d, h, r):
        k = SUMS.index((d, h, r))
        return remote(rs_send.at[k], rs_recv.at[k], rs_sem, k, ring[d])

    def c_ss(d, h, r):
        k = SUMS.index((d, h, r))
        return remote(ss_send.at[k], ss_recv.at[k], ss_sem, k, ring[d])

    def c_fin(k):
        if k == 0:
            return remote(fin_send, fin_recv, fin_sem, 0, far)
        src = rest_send.at[0, 1 - u] if k == 1 else rest_send.at[1, u if k == 2 else 1 - u]
        return remote(src, rest_recv.at[k - 1], fin_sem, k, (far, quad[2], cross)[k - 1])

    def c_ara(k):
        return remote(arw.at[xs[k]], ar_recv.at[k - 1], ar_sem, k - 1, xdev[k])

    def c_arb():
        return remote(ar_mid, ar_mid_recv, ar_sem, 3, ydev)

    def c_arc(k):
        return remote(ar_tot.at[ix], ar_tot.at[ix], ar_sem, 3 + k, xdev[k])

    def c_arc_recv(k):
        src = xs[NX - k]
        return remote(ar_tot.at[src], ar_tot.at[src], ar_sem, 3 + k, xdev[k])

    loads[0].wait()
    wbuf[u, z] = inner_v[frag[1]].astype(jnp.bfloat16)
    pl.semaphore_wait(barrier, len(partners))

    def product(lhs, members):
        g = gbuf[0:members].reshape(members * TOK, KV)
        return jnp.dot(lhs, g, preferred_element_type=jnp.float32)

    def pair_part(h, o):
        for r in (2, 3):
            c_x(r, h, o).wait_recv()
        return product(jnp.concatenate([xbuf[r, half[h], zoff(o), 0:PAIR] for r in range(4)], axis=1), 4)

    def rest_part(b, o):
        if b == 0:
            lhs = [xbuf[r, :, zoff(o), PAIR:ROWS] for r in range(2)]
        else:
            lhs = [xrest[r, :, zoff(o)] for r in range(2)]
        return product(jnp.concatenate([v.reshape(2 * REST, TOK) for v in lhs], axis=1), 2)

    def add_and_send(part, copy, send, recv, d, h, r):
        mine = part(h, DIRS[d] * (HALF - r))
        if (d, h, r - 1) in SUMS:
            copy(d, h, r - 1).wait_recv()
            mine = mine + recv[SUMS.index((d, h, r - 1))].astype(jnp.float32)
        send[SUMS.index((d, h, r))] = mine.astype(jnp.bfloat16)
        start(copy(d, h, r))

    def last_sum(part, copy, recv, h):
        total = part(h, 0)
        for d in range(2):
            copy(d, h, HALF - 1).wait_recv()
            total = total + recv[SUMS.index((d, h, HALF - 1))].astype(jnp.float32)
        return total

    def do(op, *i):
        if op == "A0":
            for d in range(2):
                start(c_ag(d, 0, 0))
        elif op == "W":
            start(c_w())
        elif op == "FW":
            c_w_recv().wait_recv()
            for d in range(2):
                start(c_ag(d, 1, 0))
        elif op == "G":
            start(c_g(i[0]))
        elif op == "X1":
            start(c_x1(i[0]))
        elif op == "GS":
            c_g(1).wait_recv()
            loads[5].wait()
            c_x1(0).wait_recv()
        elif op == "G3":
            c_g(2).wait_recv()
            start(c_g(3))
        elif op == "GP":
            c_g(3).wait_recv()
            gt[...] = gbuf[...].reshape(4 * TOK, KV).T
        elif op == "X0":
            loads[2].wait()
            c_x1(1).wait_recv()
        elif op == "X":
            for r in (2, 3):
                start(c_x(r, *i))
        elif op == "s":
            add_and_send(rest_part, c_ss, ss_send, ss_recv, *i)
        elif op == "S":
            add_and_send(pair_part, c_rs, rs_send, rs_recv, *i)
        elif op == "l":
            total = last_sum(rest_part, c_ss, ss_recv, i[0]).reshape(2, REST, KV)
            if i[0] == 0:
                rest_tot[...] = total
            rest_send[i[0]] = total.astype(jnp.bfloat16)
            for k in ((1,), (2, 3))[i[0]]:
                start(c_fin(k))
        elif op == "L":
            total = last_sum(pair_part, c_rs, rs_recv, i[0])
            if i[0] == 1:
                fin_send[...] = total.astype(jnp.bfloat16)
                start(c_fin(0))
            else:
                wg_out[0:PAIR] = total
        elif op == "F":
            d, h, j = i
            if (d, h, j - 1) in MESSAGES:
                c_ag_recv(d, h, j - 1).wait_recv()
            if (d, h, j) in MESSAGES:
                start(c_ag(d, h, j))
        elif op == "C":
            o = i[0]
            rows = wbuf[:, zoff(o)].reshape(2 * ROWS, KV)
            out = jnp.dot(rows, gt[...], preferred_element_type=jnp.float32).astype(jnp.bfloat16)
            for r in range(1, 4):
                osend[r, o % NZ] = out[:, r * TOK:(r + 1) * TOK].reshape(2, ROWS, TOK)
            for r in (2, 3, 1):
                start(c_o(r, o))
            ig_out[:, p, zoff(o), core] = out[:, :TOK].reshape(2, ROWS, TOK)
        elif op == "R1":
            loads[3].wait()
            weighted = (outer_v[...] - inner_v[frag[0]]) / 8.0
            for k in range(NX):
                arw[k] = weighted[:, k * 128:(k + 1) * 128]
            for k in range(1, NX):
                start(c_ara(k))
        elif op == "R2":
            for k in range(1, NX):
                c_ara(k).wait_recv()
            ar_mid[...] = arw[ix] + ar_recv[0] + ar_recv[1] + ar_recv[2]
            start(c_arb())
        elif op == "R3":
            c_arb().wait_recv()
            ar_tot[ix] = ar_mid[...] + ar_mid_recv[...]
            for k in range(1, NX):
                start(c_arc(k))
        elif op == "R4":
            for k in range(1, NX):
                c_arc_recv(k).wait_recv()
            loads[4].wait()
            for k in range(NX):
                cols = slice(k * 128, (k + 1) * 128)
                delta = ar_tot[k]
                new_momentum = 0.9 * mom_v[:, cols] + delta
                newmom_out[:, cols] = new_momentum
                par_out[:, cols] = outer_v[:, cols] - 0.7 * (delta + 0.9 * new_momentum)

    loads[1].wait()
    for step in PLAN:
        do(*step)

    for k in range(4):
        c_fin(k).wait_recv()
    wg_out[0:PAIR] += fin_recv[...].astype(jnp.float32)
    rest = rest_tot[u]
    for k in range(3):
        rest = rest + rest_recv[k].astype(jnp.float32)
    wg_out[PAIR:ROWS] = rest
    for o in range(-3, 5):
        for r in (1, 2, 3):
            c_o_recv(r, o).wait_recv()
    for c in sent:
        c.wait_send()


def local(act_t, cotangent, inner_params, outer_params, momentum, frag_index):
    bf16, f32 = jnp.bfloat16, jnp.float32
    hbm = pl.BlockSpec(memory_space=pltpu.HBM)
    vmem = pl.BlockSpec(memory_space=pltpu.VMEM)
    shape6 = (2, 2, NZ, 2, ROWS, TOK)
    dma = pltpu.SemaphoreType.DMA
    results, ig = pl.pallas_call(
        kernel,
        out_shape=(
            pltpu.VMEM((3, ROWS, KV), f32),
            pltpu.VMEM(shape6, bf16),
        ),
        in_specs=[pl.BlockSpec(memory_space=pltpu.SMEM)] + [hbm] * 5,
        out_specs=(vmem, vmem),
        scratch_shapes=[
            pltpu.VMEM((4, ROWS, KV), f32),
            pltpu.VMEM((ROWS, KV), f32),
            pltpu.VMEM((ROWS, KV), f32),
            pltpu.VMEM((4, TOK, KV), bf16),
            pltpu.VMEM((KV, 4 * TOK), bf16),
            pltpu.VMEM((4, 2, NZ, ROWS, TOK), bf16),
            pltpu.VMEM((2, 2, NZ, REST, TOK), bf16),
            pltpu.VMEM((2, NZ, ROWS, KV), bf16),
            pltpu.VMEM((4, NZ, 2, ROWS, TOK), bf16),
            pltpu.VMEM((len(SUMS), PAIR, KV), bf16),
            pltpu.VMEM((len(SUMS), PAIR, KV), bf16),
            pltpu.VMEM((PAIR, KV), bf16),
            pltpu.VMEM((PAIR, KV), bf16),
            pltpu.VMEM((len(SUMS), 2 * REST, KV), bf16),
            pltpu.VMEM((len(SUMS), 2 * REST, KV), bf16),
            pltpu.VMEM((2, REST, KV), f32),
            pltpu.VMEM((2, 2, REST, KV), bf16),
            pltpu.VMEM((3, REST, KV), bf16),
            pltpu.VMEM((NX, ROWS, 128), f32),
            pltpu.VMEM((NX - 1, ROWS, 128), f32),
            pltpu.VMEM((ROWS, 128), f32),
            pltpu.VMEM((ROWS, 128), f32),
            pltpu.VMEM((NX, ROWS, 128), f32),
            dma((6,)),
            dma((2, 1)),
            dma((2, 3)),
            dma((2, len(MESSAGES))),
            dma((2, 2 + 4 * NZ)),
            dma((2, 3 * NZ)),
            dma((2, len(SUMS))),
            dma((2, len(SUMS))),
            dma((2, 4)),
            dma((2, 7)),
        ],
        compiler_params=pltpu.CompilerParams(
            collective_id=0, has_side_effects=True, vmem_limit_bytes=56 * 2**20
        ),
        cost_estimate=pl.CostEstimate(flops=1700000000, bytes_accessed=6000000, transcendentals=0),
    )(
        frag_index,
        act_t.reshape(shape6),
        cotangent,
        inner_params,
        outer_params,
        momentum,
    )
    wg, par, newmom = results[0], results[1], results[2]
    return wg[None], ig.reshape(act_t.shape), par, newmom


def solution(mesh):
    in_specs = (
        P(None, ("island", "fsdp")),
        P(("island", "fsdp"), None),
        P("island", None, "fsdp", None),
        P("fsdp", None),
        P("fsdp", None),
        P(),
    )
    out_specs = (
        P("island", "fsdp", None),
        P(None, ("island", "fsdp")),
        P("fsdp", None),
        P("fsdp", None),
    )
    return jax.shard_map(local, mesh=mesh, in_specs=in_specs, out_specs=out_specs, check_vma=False)
```

```python
import jax
import jax.numpy as jnp
from jax import lax
from jax.experimental import pallas as pl
from jax.experimental.pallas import tpu as pltpu
from jax.sharding import PartitionSpec as P

MESH = pl.DeviceIdType.MESH
KV = 512
TOK = 128
ROWS = 96
NZ = 8
NX = 4
HALF = NZ // 2
DIRS = (1, -1)


def chain(d, h):
    return HALF if d == h else HALF - 1


MESSAGES = [(d, h, j) for d in range(2) for h in range(2) for j in range(HALF) if j < chain(d, h)]
SUMS = [(d, h, r) for d in range(2) for h in range(2) for r in range(HALF) if HALF - r <= chain(d, h)]
PAIR = 64
REST = ROWS - PAIR

PLAN = (
    ("W",), ("G", 1), ("X1", 0), ("X", 0, -3), ("Z",), ("A0",), ("X1", 1), ("G", 2), ("X", 1, 4),
    ("X", 1, -2), ("GS",), ("s", 1, 1, 0), ("s", 0, 1, 1), ("R1",), ("X0",), ("X", 0, -2), ("s", 0, 0, 0),
    ("s", 1, 0, 1), ("F", 1, 0, 1), ("X", 1, -3), ("F", 0, 0, 1), ("X", 1, 3), ("X", 0, 3), ("FW",),
    ("s", 1, 1, 1), ("X", 1, 2), ("s", 0, 0, 1), ("R2",), ("G3",), ("X", 1, 0), ("X", 0, 4), ("s", 0, 1, 2),
    ("F", 1, 0, 2), ("X", 0, 1), ("F", 0, 0, 2), ("X", 0, 2), ("GP",), ("S", 1, 1, 0), ("X", 1, -1),
    ("F", 1, 1, 1), ("X", 0, 0), ("S", 0, 1, 1), ("X", 1, 1), ("C", 1), ("s", 0, 0, 2), ("s", 0, 1, 3),
    ("F", 0, 1, 1), ("S", 0, 0, 0), ("S", 1, 1, 1), ("s", 1, 1, 2), ("C", 0), ("X", 0, -1), ("F", 1, 1, 2),
    ("R3",), ("C", -1), ("C", 2), ("S", 1, 1, 2), ("S", 0, 1, 2), ("F", 0, 0, 3), ("s", 1, 1, 3),
    ("S", 1, 0, 1), ("s", 1, 0, 2), ("F", 0, 1, 2), ("F", 1, 1, 3), ("C", -2), ("F", 1, 0, 3),
    ("S", 0, 0, 1), ("R4",), ("l", 1), ("S", 0, 1, 3), ("C", 3), ("S", 1, 1, 3), ("s", 0, 0, 3),
    ("s", 1, 0, 3), ("F", 0, 1, 3), ("F", 0, 0, 4), ("C", -3), ("S", 1, 0, 2), ("S", 0, 0, 2),
    ("F", 1, 1, 4), ("L", 1), ("l", 0), ("C", 4), ("S", 0, 0, 3), ("S", 1, 0, 3), ("L", 0),
)


def kernel(
    frag, x_hbm, g_hbm, inner_hbm, outer_hbm, mom_hbm,
    f_out, ig_out,
    inner_v, outer_v, mom_v, gbuf, gt, xbuf, xrest, wbuf, osend, rs_send, rs_recv, fin_send, fin_recv,
    ss_send, ss_recv, rest_tot, rest_send, rest_recv,
    arw, ar_recv, ar_mid, ar_mid_recv, ar_tot,
    local_sem, w_sem, g_sem, ag_sem, x_sem, o_sem, rs_sem, ss_sem, fin_sem, ar_sem, ready,
):
    wg_out, par_out, newmom_out = (f_out.at[k] for k in range(3))
    island = lax.axis_index("island")
    me = lax.axis_index("fsdp")
    core = lax.rem(me, 2)
    z = lax.rem(me // 2, NZ)
    y = me // (2 * NZ)
    u = y // 2
    p = lax.rem(y, 2)
    half = (u, 1 - u)
    ix = island // 2
    iy = lax.rem(island, 2)

    def at(yy, zz, cc):
        return (island, (yy * NZ + zz) * 2 + cc)

    def zoff(o):
        return lax.rem(z + (o + NZ), NZ)

    y_pair = y + 1 - 2 * p
    quad = [None, at(y, z, 1 - core), at(y_pair, z, core), at(y_pair, z, 1 - core)]
    quad_pc = [(p, core), (p, 1 - core), (1 - p, core), (1 - p, 1 - core)]
    far = at(lax.rem(y + 2, 4), z, core)
    cross = at(3 - y, z, core)
    ring = [at(y, zoff(1), core), at(y, zoff(-1), core)]
    xs = [lax.rem(ix + k, NX) for k in range(NX)]
    xdev = [None] + [(xs[k] * 2 + iy, me) for k in range(1, NX)]
    ydev = (ix * 2 + 1 - iy, me)

    loads = [
        pltpu.make_async_copy(inner_hbm.at[0], inner_v, local_sem.at[0]),
        pltpu.make_async_copy(g_hbm, gbuf.at[0], local_sem.at[1]),
        pltpu.make_async_copy(x_hbm.at[:, p, :, core], xbuf.at[0], local_sem.at[2]),
        pltpu.make_async_copy(outer_hbm, outer_v, local_sem.at[3]),
        pltpu.make_async_copy(mom_hbm, mom_v, local_sem.at[4]),
        pltpu.make_async_copy(x_hbm.at[:, 1 - p, :, core, PAIR:], xrest.at[0], local_sem.at[5]),
    ]
    for c in loads:
        c.start()

    barrier = pltpu.get_barrier_semaphore()
    def signal(sem, dev):
        pl.semaphore_signal(sem, inc=1, device_id=dev, device_id_type=MESH)

    partners = quad[1:] + [far, cross] + xdev[1:]
    for dev in partners:
        signal(barrier, dev)

    @pl.when(z < NZ - 1)
    def _():
        signal(barrier, ring[0])

    @pl.when(z == 0)
    def _():
        signal(barrier, ring[1])

    @pl.when(iy == 0)
    def _():
        signal(barrier, ydev)

    after_z = jnp.minimum(z, 1)
    at_end = z // (NZ - 1)

    sent = []

    def remote(src, dst, sems, k, dev):
        return pltpu.make_async_remote_copy(
            src_ref=src, dst_ref=dst, send_sem=sems.at[0, k], recv_sem=sems.at[1, k],
            device_id=dev, device_id_type=MESH,
        )

    def start(c):
        c.start()
        sent.append(c)

    def c_w():
        return remote(wbuf.at[u, z], wbuf.at[u, z], w_sem, 0, far)

    def c_w_recv():
        return remote(wbuf.at[1 - u, z], wbuf.at[1 - u, z], w_sem, 0, far)

    def c_g(r):
        src, dst, dev = ((0, 1, quad[1]), (0, 2, quad[2]), (2, 3, quad[1]))[r - 1]
        return remote(gbuf.at[src], gbuf.at[dst], g_sem, r - 1, dev)

    def c_ag(d, h, j):
        zz = zoff(-DIRS[d] * j)
        return remote(wbuf.at[half[h], zz], wbuf.at[half[h], zz], ag_sem, MESSAGES.index((d, h, j)), ring[d])

    def c_ag_recv(d, h, j):
        zz = zoff(-DIRS[d] * (j + 1))
        return remote(wbuf.at[half[h], zz], wbuf.at[half[h], zz], ag_sem, MESSAGES.index((d, h, j)), ring[d])

    def c_x1(k):
        if k == 0:
            return remote(x_hbm.at[:, 1 - p, :, 1 - core, PAIR:], xrest.at[1], x_sem, 0, quad[1])
        return remote(x_hbm.at[:, p, :, 1 - core], xbuf.at[1], x_sem, 1, quad[1])

    def c_x(r, h, o):
        pp, cc = quad_pc[r]
        zz = zoff(o)
        k = 2 + ((r - 2) * 2 + h) * NZ + o % NZ
        rows = pl.ds(0, PAIR)
        return remote(x_hbm.at[half[h], pp, zz, cc, rows], xbuf.at[r, half[h], zz, rows], x_sem, k, quad[r])

    def c_o(r, o):
        zz = zoff(o)
        return remote(osend.at[r, o % NZ], ig_out.at[:, p, zz, core], o_sem, (r - 1) * NZ + o % NZ, quad[r])

    def c_o_recv(r, o):
        pp, cc = quad_pc[r]
        zz = zoff(o)
        return remote(osend.at[r, o % NZ], ig_out.at[:, pp, zz, cc], o_sem, (r - 1) * NZ + o % NZ, quad[r])

    def c_rs(d, h, r):
        k = SUMS.index((d, h, r))
        return remote(rs_send.at[k], rs_recv.at[k], rs_sem, k, ring[d])

    def c_ss(d, h, r):
        k = SUMS.index((d, h, r))
        return remote(ss_send.at[k], ss_recv.at[k], ss_sem, k, ring[d])

    def c_fin(k):
        if k == 0:
            return remote(fin_send, fin_recv, fin_sem, 0, far)
        src = rest_send.at[0, 1 - u] if k == 1 else rest_send.at[1, u if k == 2 else 1 - u]
        return remote(src, rest_recv.at[k - 1], fin_sem, k, (far, quad[2], cross)[k - 1])

    def c_ara(k):
        return remote(arw.at[xs[k]], ar_recv.at[k - 1], ar_sem, k - 1, xdev[k])

    def c_arb():
        return remote(ar_mid, ar_mid_recv, ar_sem, 3, ydev)

    def c_arc(k):
        return remote(ar_tot.at[ix], ar_tot.at[ix], ar_sem, 3 + k, xdev[k])

    def c_arc_recv(k):
        src = xs[NX - k]
        return remote(ar_tot.at[src], ar_tot.at[src], ar_sem, 3 + k, xdev[k])

    loads[0].wait()
    wbuf[u, z] = inner_v[frag[1]].astype(jnp.bfloat16)
    pl.semaphore_wait(barrier, len(partners) + after_z + at_end + iy)

    @pl.when(z > 0)
    def _():
        signal(ready.at[0], ring[1])

    @pl.when(z == NZ - 1)
    def _():
        signal(ready.at[1], ring[0])

    @pl.when(iy == 1)
    def _():
        signal(ready.at[2], ydev)


    def product(lhs, members):
        g = gbuf[0:members].reshape(members * TOK, KV)
        return jnp.dot(lhs, g, preferred_element_type=jnp.float32)

    def pair_part(h, o):
        for r in (2, 3):
            c_x(r, h, o).wait_recv()
        return product(jnp.concatenate([xbuf[r, half[h], zoff(o), 0:PAIR] for r in range(4)], axis=1), 4)

    def rest_part(b, o):
        if b == 0:
            lhs = [xbuf[r, :, zoff(o), PAIR:ROWS] for r in range(2)]
        else:
            lhs = [xrest[r, :, zoff(o)] for r in range(2)]
        return product(jnp.concatenate([v.reshape(2 * REST, TOK) for v in lhs], axis=1), 2)

    def add_and_send(part, copy, send, recv, d, h, r):
        mine = part(h, DIRS[d] * (HALF - r))
        if (d, h, r - 1) in SUMS:
            copy(d, h, r - 1).wait_recv()
            mine = mine + recv[SUMS.index((d, h, r - 1))].astype(jnp.float32)
        send[SUMS.index((d, h, r))] = mine.astype(jnp.bfloat16)
        start(copy(d, h, r))

    def last_sum(part, copy, recv, h):
        total = part(h, 0)
        for d in range(2):
            copy(d, h, HALF - 1).wait_recv()
            total = total + recv[SUMS.index((d, h, HALF - 1))].astype(jnp.float32)
        return total

    def do(op, *i):
        if op == "Z":
            @pl.when(z < NZ - 1)
            def _():
                pl.semaphore_wait(ready.at[0], 1)

            @pl.when(z == 0)
            def _():
                pl.semaphore_wait(ready.at[1], 1)
        elif op == "A0":
            for d in range(2):
                start(c_ag(d, 0, 0))
        elif op == "W":
            start(c_w())
        elif op == "FW":
            c_w_recv().wait_recv()
            for d in range(2):
                start(c_ag(d, 1, 0))
        elif op == "G":
            start(c_g(i[0]))
        elif op == "X1":
            start(c_x1(i[0]))
        elif op == "GS":
            c_g(1).wait_recv()
            loads[5].wait()
            c_x1(0).wait_recv()
        elif op == "G3":
            c_g(2).wait_recv()
            start(c_g(3))
        elif op == "GP":
            c_g(3).wait_recv()
            gt[...] = gbuf[...].reshape(4 * TOK, KV).T
        elif op == "X0":
            loads[2].wait()
            c_x1(1).wait_recv()
        elif op == "X":
            for r in (2, 3):
                start(c_x(r, *i))
        elif op == "s":
            add_and_send(rest_part, c_ss, ss_send, ss_recv, *i)
        elif op == "S":
            add_and_send(pair_part, c_rs, rs_send, rs_recv, *i)
        elif op == "l":
            total = last_sum(rest_part, c_ss, ss_recv, i[0]).reshape(2, REST, KV)
            if i[0] == 0:
                rest_tot[...] = total
            rest_send[i[0]] = total.astype(jnp.bfloat16)
            for k in ((1,), (2, 3))[i[0]]:
                start(c_fin(k))
        elif op == "L":
            total = last_sum(pair_part, c_rs, rs_recv, i[0])
            if i[0] == 1:
                fin_send[...] = total.astype(jnp.bfloat16)
                start(c_fin(0))
            else:
                wg_out[0:PAIR] = total
        elif op == "F":
            d, h, j = i
            if (d, h, j - 1) in MESSAGES:
                c_ag_recv(d, h, j - 1).wait_recv()
            if (d, h, j) in MESSAGES:
                start(c_ag(d, h, j))
        elif op == "C":
            o = i[0]
            rows = wbuf[:, zoff(o)].reshape(2 * ROWS, KV)
            out = jnp.dot(rows, gt[...], preferred_element_type=jnp.float32).astype(jnp.bfloat16)
            for r in range(1, 4):
                osend[r, o % NZ] = out[:, r * TOK:(r + 1) * TOK].reshape(2, ROWS, TOK)
            for r in (2, 3, 1):
                start(c_o(r, o))
            ig_out[:, p, zoff(o), core] = out[:, :TOK].reshape(2, ROWS, TOK)
        elif op == "R1":
            loads[3].wait()
            weighted = (outer_v[...] - inner_v[frag[0]]) / 8.0
            for k in range(NX):
                arw[k] = weighted[:, k * 128:(k + 1) * 128]
            for k in range(1, NX):
                start(c_ara(k))
        elif op == "R2":
            for k in range(1, NX):
                c_ara(k).wait_recv()
            ar_mid[...] = arw[ix] + ar_recv[0] + ar_recv[1] + ar_recv[2]

            @pl.when(iy == 0)
            def _():
                pl.semaphore_wait(ready.at[2], 1)

            start(c_arb())
        elif op == "R3":
            c_arb().wait_recv()
            ar_tot[ix] = ar_mid[...] + ar_mid_recv[...]
            for k in range(1, NX):
                start(c_arc(k))
        elif op == "R4":
            for k in range(1, NX):
                c_arc_recv(k).wait_recv()
            loads[4].wait()
            for k in range(NX):
                cols = slice(k * 128, (k + 1) * 128)
                delta = ar_tot[k]
                new_momentum = 0.9 * mom_v[:, cols] + delta
                newmom_out[:, cols] = new_momentum
                par_out[:, cols] = outer_v[:, cols] - 0.7 * (delta + 0.9 * new_momentum)

    loads[1].wait()
    for step in PLAN:
        do(*step)

    for k in range(4):
        c_fin(k).wait_recv()
    wg_out[0:PAIR] += fin_recv[...].astype(jnp.float32)
    rest = rest_tot[u]
    for k in range(3):
        rest = rest + rest_recv[k].astype(jnp.float32)
    wg_out[PAIR:ROWS] = rest
    for o in range(-3, 5):
        for r in (1, 2, 3):
            c_o_recv(r, o).wait_recv()
    for c in sent:
        c.wait_send()


def local(act_t, cotangent, inner_params, outer_params, momentum, frag_index):
    bf16, f32 = jnp.bfloat16, jnp.float32
    hbm = pl.BlockSpec(memory_space=pltpu.HBM)
    vmem = pl.BlockSpec(memory_space=pltpu.VMEM)
    shape6 = (2, 2, NZ, 2, ROWS, TOK)
    dma = pltpu.SemaphoreType.DMA
    results, ig = pl.pallas_call(
        kernel,
        out_shape=(
            pltpu.VMEM((3, ROWS, KV), f32),
            pltpu.VMEM(shape6, bf16),
        ),
        in_specs=[pl.BlockSpec(memory_space=pltpu.SMEM)] + [hbm] * 5,
        out_specs=(vmem, vmem),
        scratch_shapes=[
            pltpu.VMEM((4, ROWS, KV), f32),
            pltpu.VMEM((ROWS, KV), f32),
            pltpu.VMEM((ROWS, KV), f32),
            pltpu.VMEM((4, TOK, KV), bf16),
            pltpu.VMEM((KV, 4 * TOK), bf16),
            pltpu.VMEM((4, 2, NZ, ROWS, TOK), bf16),
            pltpu.VMEM((2, 2, NZ, REST, TOK), bf16),
            pltpu.VMEM((2, NZ, ROWS, KV), bf16),
            pltpu.VMEM((4, NZ, 2, ROWS, TOK), bf16),
            pltpu.VMEM((len(SUMS), PAIR, KV), bf16),
            pltpu.VMEM((len(SUMS), PAIR, KV), bf16),
            pltpu.VMEM((PAIR, KV), bf16),
            pltpu.VMEM((PAIR, KV), bf16),
            pltpu.VMEM((len(SUMS), 2 * REST, KV), bf16),
            pltpu.VMEM((len(SUMS), 2 * REST, KV), bf16),
            pltpu.VMEM((2, REST, KV), f32),
            pltpu.VMEM((2, 2, REST, KV), bf16),
            pltpu.VMEM((3, REST, KV), bf16),
            pltpu.VMEM((NX, ROWS, 128), f32),
            pltpu.VMEM((NX - 1, ROWS, 128), f32),
            pltpu.VMEM((ROWS, 128), f32),
            pltpu.VMEM((ROWS, 128), f32),
            pltpu.VMEM((NX, ROWS, 128), f32),
            dma((6,)),
            dma((2, 1)),
            dma((2, 3)),
            dma((2, len(MESSAGES))),
            dma((2, 2 + 4 * NZ)),
            dma((2, 3 * NZ)),
            dma((2, len(SUMS))),
            dma((2, len(SUMS))),
            dma((2, 4)),
            dma((2, 7)),
            pltpu.SemaphoreType.REGULAR((3,)),
        ],
        compiler_params=pltpu.CompilerParams(
            collective_id=0, has_side_effects=True, vmem_limit_bytes=56 * 2**20
        ),
        cost_estimate=pl.CostEstimate(flops=1700000000, bytes_accessed=6000000, transcendentals=0),
    )(
        frag_index,
        act_t.reshape(shape6),
        cotangent,
        inner_params,
        outer_params,
        momentum,
    )
    wg, par, newmom = results[0], results[1], results[2]
    return wg[None], ig.reshape(act_t.shape), par, newmom


def solution(mesh):
    in_specs = (
        P(None, ("island", "fsdp")),
        P(("island", "fsdp"), None),
        P("island", None, "fsdp", None),
        P("fsdp", None),
        P("fsdp", None),
        P(),
    )
    out_specs = (
        P("island", "fsdp", None),
        P(None, ("island", "fsdp")),
        P("fsdp", None),
        P("fsdp", None),
    )
    return jax.shard_map(local, mesh=mesh, in_specs=in_specs, out_specs=out_specs, check_vma=False)
```

```python
import jax
import jax.numpy as jnp
from jax import lax
from jax.experimental import pallas as pl
from jax.experimental.pallas import tpu as pltpu
from jax.sharding import PartitionSpec as P

MESH = pl.DeviceIdType.MESH
KV = 512
TOK = 128
ROWS = 96
NZ = 8
NX = 4
HALF = NZ // 2
DIRS = (1, -1)


def chain(d, h):
    return HALF if d == h else HALF - 1


MESSAGES = [(d, h, j) for d in range(2) for h in range(2) for j in range(HALF) if j < chain(d, h)]
SUMS = [(d, h, r) for d in range(2) for h in range(2) for r in range(HALF) if HALF - r <= chain(d, h)]
PAIR = 64
REST = ROWS - PAIR

PLAN = (
    ("G", 1), ("X1", 0), ("X", 0, -3), ("W",), ("Z",), ("A0",), ("X1", 1), ("G", 2), ("X", 1, 4),
    ("X", 1, -2), ("GS",), ("s", 1, 1, 0), ("s", 0, 1, 1), ("R1",), ("X0",), ("X", 0, -2), ("s", 0, 0, 0),
    ("s", 1, 0, 1), ("F", 1, 0, 1), ("X", 1, -3), ("F", 0, 0, 1), ("X", 1, 3), ("X", 0, 3), ("FW",),
    ("s", 1, 1, 1), ("X", 1, 2), ("s", 0, 0, 1), ("R2",), ("G3",), ("X", 1, 0), ("X", 0, 4), ("s", 0, 1, 2),
    ("F", 1, 0, 2), ("X", 0, 1), ("F", 0, 0, 2), ("X", 0, 2), ("GP",), ("S", 1, 1, 0), ("X", 1, -1),
    ("F", 1, 1, 1), ("X", 0, 0), ("S", 0, 1, 1), ("X", 1, 1), ("C", 1), ("s", 0, 0, 2), ("s", 0, 1, 3),
    ("F", 0, 1, 1), ("S", 0, 0, 0), ("S", 1, 1, 1), ("s", 1, 1, 2), ("C", 0), ("X", 0, -1), ("F", 1, 1, 2),
    ("C", -1), ("C", 2), ("S", 1, 1, 2), ("S", 0, 1, 2), ("F", 0, 0, 3), ("s", 1, 1, 3),
    ("S", 1, 0, 1), ("s", 1, 0, 2), ("F", 0, 1, 2), ("F", 1, 1, 3), ("C", -2), ("R3",), ("F", 1, 0, 3),
    ("S", 0, 0, 1), ("l", 1), ("S", 0, 1, 3), ("C", 3), ("S", 1, 1, 3), ("s", 0, 0, 3),
    ("s", 1, 0, 3), ("F", 0, 1, 3), ("F", 0, 0, 4), ("C", -3), ("S", 1, 0, 2), ("S", 0, 0, 2),
    ("F", 1, 1, 4), ("L", 1), ("l", 0), ("C", 4), ("R4",), ("S", 0, 0, 3), ("S", 1, 0, 3), ("L", 0),
)


def kernel(
    frag, x_hbm, g_hbm, inner_hbm, outer_hbm, mom_hbm,
    f_out, ig_out,
    inner_v, outer_v, mom_v, gbuf, gt, xbuf, xrest, wbuf, osend, rs_send, rs_recv, fin_send, fin_recv,
    ss_send, ss_recv, rest_tot, rest_send, rest_recv,
    arw, ar_recv, ar_mid, ar_mid_recv, ar_tot,
    local_sem, w_sem, g_sem, ag_sem, x_sem, o_sem, rs_sem, ss_sem, fin_sem, ar_sem, ready,
):
    wg_out, par_out, newmom_out = (f_out.at[k] for k in range(3))
    island = lax.axis_index("island")
    me = lax.axis_index("fsdp")
    core = lax.rem(me, 2)
    z = lax.rem(me // 2, NZ)
    y = me // (2 * NZ)
    u = y // 2
    p = lax.rem(y, 2)
    half = (u, 1 - u)
    ix = island // 2
    iy = lax.rem(island, 2)

    def at(yy, zz, cc):
        return (island, (yy * NZ + zz) * 2 + cc)

    def zoff(o):
        return lax.rem(z + (o + NZ), NZ)

    y_pair = y + 1 - 2 * p
    quad = [None, at(y, z, 1 - core), at(y_pair, z, core), at(y_pair, z, 1 - core)]
    quad_pc = [(p, core), (p, 1 - core), (1 - p, core), (1 - p, 1 - core)]
    far = at(lax.rem(y + 2, 4), z, core)
    cross = at(3 - y, z, core)
    ring = [at(y, zoff(1), core), at(y, zoff(-1), core)]
    xs = [lax.rem(ix + k, NX) for k in range(NX)]
    xdev = [None] + [(xs[k] * 2 + iy, me) for k in range(1, NX)]
    ydev = (ix * 2 + 1 - iy, me)

    loads = [
        pltpu.make_async_copy(inner_hbm.at[0], inner_v, local_sem.at[0]),
        pltpu.make_async_copy(g_hbm, gbuf.at[0], local_sem.at[1]),
        pltpu.make_async_copy(x_hbm.at[:, p, :, core], xbuf.at[0], local_sem.at[2]),
        pltpu.make_async_copy(outer_hbm, outer_v, local_sem.at[3]),
        pltpu.make_async_copy(mom_hbm, mom_v, local_sem.at[4]),
        pltpu.make_async_copy(x_hbm.at[:, 1 - p, :, core, PAIR:], xrest.at[0], local_sem.at[5]),
    ]
    for c in loads:
        c.start()

    barrier = pltpu.get_barrier_semaphore()
    def signal(sem, dev):
        pl.semaphore_signal(sem, inc=1, device_id=dev, device_id_type=MESH)

    partners = quad[1:] + [far, cross] + xdev[1:]
    for dev in partners:
        signal(barrier, dev)

    @pl.when(z < NZ - 1)
    def _():
        signal(barrier, ring[0])

    @pl.when(z == 0)
    def _():
        signal(barrier, ring[1])

    @pl.when(iy == 0)
    def _():
        signal(barrier, ydev)

    after_z = jnp.minimum(z, 1)
    at_end = z // (NZ - 1)

    sent = []

    def remote(src, dst, sems, k, dev):
        return pltpu.make_async_remote_copy(
            src_ref=src, dst_ref=dst, send_sem=sems.at[0, k], recv_sem=sems.at[1, k],
            device_id=dev, device_id_type=MESH,
        )

    def start(c):
        c.start()
        sent.append(c)

    def c_w():
        return remote(wbuf.at[u, z], wbuf.at[u, z], w_sem, 0, far)

    def c_w_recv():
        return remote(wbuf.at[1 - u, z], wbuf.at[1 - u, z], w_sem, 0, far)

    def c_g(r):
        src, dst, dev = ((0, 1, quad[1]), (0, 2, quad[2]), (2, 3, quad[1]))[r - 1]
        return remote(gbuf.at[src], gbuf.at[dst], g_sem, r - 1, dev)

    def c_ag(d, h, j):
        zz = zoff(-DIRS[d] * j)
        return remote(wbuf.at[half[h], zz], wbuf.at[half[h], zz], ag_sem, MESSAGES.index((d, h, j)), ring[d])

    def c_ag_recv(d, h, j):
        zz = zoff(-DIRS[d] * (j + 1))
        return remote(wbuf.at[half[h], zz], wbuf.at[half[h], zz], ag_sem, MESSAGES.index((d, h, j)), ring[d])

    def c_x1(k):
        if k == 0:
            return remote(x_hbm.at[:, 1 - p, :, 1 - core, PAIR:], xrest.at[1], x_sem, 0, quad[1])
        return remote(x_hbm.at[:, p, :, 1 - core], xbuf.at[1], x_sem, 1, quad[1])

    def c_x(r, h, o):
        pp, cc = quad_pc[r]
        zz = zoff(o)
        k = 2 + ((r - 2) * 2 + h) * NZ + o % NZ
        rows = pl.ds(0, PAIR)
        return remote(x_hbm.at[half[h], pp, zz, cc, rows], xbuf.at[r, half[h], zz, rows], x_sem, k, quad[r])

    def c_o(r, o):
        zz = zoff(o)
        return remote(osend.at[r, o % NZ], ig_out.at[:, p, zz, core], o_sem, (r - 1) * NZ + o % NZ, quad[r])

    def c_o_recv(r, o):
        pp, cc = quad_pc[r]
        zz = zoff(o)
        return remote(osend.at[r, o % NZ], ig_out.at[:, pp, zz, cc], o_sem, (r - 1) * NZ + o % NZ, quad[r])

    def c_rs(d, h, r):
        k = SUMS.index((d, h, r))
        return remote(rs_send.at[k], rs_recv.at[k], rs_sem, k, ring[d])

    def c_ss(d, h, r):
        k = SUMS.index((d, h, r))
        return remote(ss_send.at[k], ss_recv.at[k], ss_sem, k, ring[d])

    def c_fin(k):
        if k == 0:
            return remote(fin_send, fin_recv, fin_sem, 0, far)
        src = rest_send.at[0, 1 - u] if k == 1 else rest_send.at[1, u if k == 2 else 1 - u]
        return remote(src, rest_recv.at[k - 1], fin_sem, k, (far, quad[2], cross)[k - 1])

    def c_ara(k):
        return remote(arw.at[xs[k]], ar_recv.at[k - 1], ar_sem, k - 1, xdev[k])

    def c_arb():
        return remote(ar_mid, ar_mid_recv, ar_sem, 3, ydev)

    def c_arc(k):
        return remote(ar_tot.at[ix], ar_tot.at[ix], ar_sem, 3 + k, xdev[k])

    def c_arc_recv(k):
        src = xs[NX - k]
        return remote(ar_tot.at[src], ar_tot.at[src], ar_sem, 3 + k, xdev[k])

    pl.semaphore_wait(barrier, len(partners) + after_z + at_end + iy)

    @pl.when(z > 0)
    def _():
        signal(ready.at[0], ring[1])

    @pl.when(z == NZ - 1)
    def _():
        signal(ready.at[1], ring[0])

    @pl.when(iy == 1)
    def _():
        signal(ready.at[2], ydev)


    def product(lhs, members):
        g = gbuf[0:members].reshape(members * TOK, KV)
        return jnp.dot(lhs, g, preferred_element_type=jnp.float32)

    def pair_part(h, o):
        for r in (2, 3):
            c_x(r, h, o).wait_recv()
        return product(jnp.concatenate([xbuf[r, half[h], zoff(o), 0:PAIR] for r in range(4)], axis=1), 4)

    def rest_part(b, o):
        if b == 0:
            lhs = [xbuf[r, :, zoff(o), PAIR:ROWS] for r in range(2)]
        else:
            lhs = [xrest[r, :, zoff(o)] for r in range(2)]
        return product(jnp.concatenate([v.reshape(2 * REST, TOK) for v in lhs], axis=1), 2)

    def add_and_send(part, copy, send, recv, d, h, r):
        mine = part(h, DIRS[d] * (HALF - r))
        if (d, h, r - 1) in SUMS:
            copy(d, h, r - 1).wait_recv()
            mine = mine + recv[SUMS.index((d, h, r - 1))].astype(jnp.float32)
        send[SUMS.index((d, h, r))] = mine.astype(jnp.bfloat16)
        start(copy(d, h, r))

    def last_sum(part, copy, recv, h):
        total = part(h, 0)
        for d in range(2):
            copy(d, h, HALF - 1).wait_recv()
            total = total + recv[SUMS.index((d, h, HALF - 1))].astype(jnp.float32)
        return total

    first_use = [step[0] for step in PLAN if step[0] in ("W", "A0", "R1")][0]

    def do(op, *i):
        if op == first_use:
            loads[0].wait()
            wbuf[u, z] = inner_v[frag[1]].astype(jnp.bfloat16)
        if op == "Z":
            @pl.when(z < NZ - 1)
            def _():
                pl.semaphore_wait(ready.at[0], 1)

            @pl.when(z == 0)
            def _():
                pl.semaphore_wait(ready.at[1], 1)
        elif op == "A0":
            for d in range(2):
                start(c_ag(d, 0, 0))
        elif op == "W":
            start(c_w())
        elif op == "FW":
            c_w_recv().wait_recv()
            for d in range(2):
                start(c_ag(d, 1, 0))
        elif op == "G":
            start(c_g(i[0]))
        elif op == "X1":
            start(c_x1(i[0]))
        elif op == "GS":
            c_g(1).wait_recv()
            loads[5].wait()
            c_x1(0).wait_recv()
        elif op == "G3":
            c_g(2).wait_recv()
            start(c_g(3))
        elif op == "GP":
            c_g(3).wait_recv()
            gt[...] = gbuf[...].reshape(4 * TOK, KV).T
        elif op == "X0":
            loads[2].wait()
            c_x1(1).wait_recv()
        elif op == "X":
            for r in (2, 3):
                start(c_x(r, *i))
        elif op == "s":
            add_and_send(rest_part, c_ss, ss_send, ss_recv, *i)
        elif op == "S":
            add_and_send(pair_part, c_rs, rs_send, rs_recv, *i)
        elif op == "l":
            total = last_sum(rest_part, c_ss, ss_recv, i[0]).reshape(2, REST, KV)
            if i[0] == 0:
                rest_tot[...] = total
            rest_send[i[0]] = total.astype(jnp.bfloat16)
            for k in ((1,), (2, 3))[i[0]]:
                start(c_fin(k))
        elif op == "L":
            total = last_sum(pair_part, c_rs, rs_recv, i[0])
            if i[0] == 1:
                fin_send[...] = total.astype(jnp.bfloat16)
                start(c_fin(0))
            else:
                wg_out[0:PAIR] = total
        elif op == "F":
            d, h, j = i
            if (d, h, j - 1) in MESSAGES:
                c_ag_recv(d, h, j - 1).wait_recv()
            if (d, h, j) in MESSAGES:
                start(c_ag(d, h, j))
        elif op == "C":
            o = i[0]
            rows = wbuf[:, zoff(o)].reshape(2 * ROWS, KV)
            out = jnp.dot(rows, gt[...], preferred_element_type=jnp.float32).astype(jnp.bfloat16)
            for r in range(1, 4):
                osend[r, o % NZ] = out[:, r * TOK:(r + 1) * TOK].reshape(2, ROWS, TOK)
            for r in (2, 3, 1):
                start(c_o(r, o))
            ig_out[:, p, zoff(o), core] = out[:, :TOK].reshape(2, ROWS, TOK)
        elif op == "R1":
            loads[3].wait()
            weighted = (outer_v[...] - inner_v[frag[0]]) / 8.0
            for k in range(NX):
                arw[k] = weighted[:, k * 128:(k + 1) * 128]
            for k in range(1, NX):
                start(c_ara(k))
        elif op == "R2":
            for k in range(1, NX):
                c_ara(k).wait_recv()
            ar_mid[...] = arw[ix] + ar_recv[0] + ar_recv[1] + ar_recv[2]

            @pl.when(iy == 0)
            def _():
                pl.semaphore_wait(ready.at[2], 1)

            start(c_arb())
        elif op == "R3":
            c_arb().wait_recv()
            ar_tot[ix] = ar_mid[...] + ar_mid_recv[...]
            for k in range(1, NX):
                start(c_arc(k))
        elif op == "R4":
            for k in range(1, NX):
                c_arc_recv(k).wait_recv()
            loads[4].wait()
            for k in range(NX):
                cols = slice(k * 128, (k + 1) * 128)
                delta = ar_tot[k]
                new_momentum = 0.9 * mom_v[:, cols] + delta
                newmom_out[:, cols] = new_momentum
                par_out[:, cols] = outer_v[:, cols] - 0.7 * (delta + 0.9 * new_momentum)

    loads[1].wait()
    for step in PLAN:
        do(*step)

    for k in range(4):
        c_fin(k).wait_recv()
    wg_out[0:PAIR] += fin_recv[...].astype(jnp.float32)
    rest = rest_tot[u]
    for k in range(3):
        rest = rest + rest_recv[k].astype(jnp.float32)
    wg_out[PAIR:ROWS] = rest
    for o in range(-3, 5):
        for r in (1, 2, 3):
            c_o_recv(r, o).wait_recv()
    for c in sent:
        c.wait_send()


def local(act_t, cotangent, inner_params, outer_params, momentum, frag_index):
    bf16, f32 = jnp.bfloat16, jnp.float32
    hbm = pl.BlockSpec(memory_space=pltpu.HBM)
    vmem = pl.BlockSpec(memory_space=pltpu.VMEM)
    shape6 = (2, 2, NZ, 2, ROWS, TOK)
    dma = pltpu.SemaphoreType.DMA
    results, ig = pl.pallas_call(
        kernel,
        out_shape=(
            pltpu.VMEM((3, ROWS, KV), f32),
            pltpu.VMEM(shape6, bf16),
        ),
        in_specs=[pl.BlockSpec(memory_space=pltpu.SMEM)] + [hbm] * 5,
        out_specs=(vmem, vmem),
        scratch_shapes=[
            pltpu.VMEM((4, ROWS, KV), f32),
            pltpu.VMEM((ROWS, KV), f32),
            pltpu.VMEM((ROWS, KV), f32),
            pltpu.VMEM((4, TOK, KV), bf16),
            pltpu.VMEM((KV, 4 * TOK), bf16),
            pltpu.VMEM((4, 2, NZ, ROWS, TOK), bf16),
            pltpu.VMEM((2, 2, NZ, REST, TOK), bf16),
            pltpu.VMEM((2, NZ, ROWS, KV), bf16),
            pltpu.VMEM((4, NZ, 2, ROWS, TOK), bf16),
            pltpu.VMEM((len(SUMS), PAIR, KV), bf16),
            pltpu.VMEM((len(SUMS), PAIR, KV), bf16),
            pltpu.VMEM((PAIR, KV), bf16),
            pltpu.VMEM((PAIR, KV), bf16),
            pltpu.VMEM((len(SUMS), 2 * REST, KV), bf16),
            pltpu.VMEM((len(SUMS), 2 * REST, KV), bf16),
            pltpu.VMEM((2, REST, KV), f32),
            pltpu.VMEM((2, 2, REST, KV), bf16),
            pltpu.VMEM((3, REST, KV), bf16),
            pltpu.VMEM((NX, ROWS, 128), f32),
            pltpu.VMEM((NX - 1, ROWS, 128), f32),
            pltpu.VMEM((ROWS, 128), f32),
            pltpu.VMEM((ROWS, 128), f32),
            pltpu.VMEM((NX, ROWS, 128), f32),
            dma((6,)),
            dma((2, 1)),
            dma((2, 3)),
            dma((2, len(MESSAGES))),
            dma((2, 2 + 4 * NZ)),
            dma((2, 3 * NZ)),
            dma((2, len(SUMS))),
            dma((2, len(SUMS))),
            dma((2, 4)),
            dma((2, 7)),
            pltpu.SemaphoreType.REGULAR((3,)),
        ],
        compiler_params=pltpu.CompilerParams(
            collective_id=0, has_side_effects=True, vmem_limit_bytes=56 * 2**20
        ),
        cost_estimate=pl.CostEstimate(flops=1700000000, bytes_accessed=6000000, transcendentals=0),
    )(
        frag_index,
        act_t.reshape(shape6),
        cotangent,
        inner_params,
        outer_params,
        momentum,
    )
    wg, par, newmom = results[0], results[1], results[2]
    return wg[None], ig.reshape(act_t.shape), par, newmom


def solution(mesh):
    in_specs = (
        P(None, ("island", "fsdp")),
        P(("island", "fsdp"), None),
        P("island", None, "fsdp", None),
        P("fsdp", None),
        P("fsdp", None),
        P(),
    )
    out_specs = (
        P("island", "fsdp", None),
        P(None, ("island", "fsdp")),
        P("fsdp", None),
        P("fsdp", None),
    )
    return jax.shard_map(local, mesh=mesh, in_specs=in_specs, out_specs=out_specs, check_vma=False)
```
